32 devices in a mesh: groups: 2 (over y), row: 8 (over z, core), col: 2 (over x), chan: 1.
Axes of the slice: x: 2, y: 2, z: 4, core: 2. Of those that a mesh axis runs over, the one named last changes fastest.
Arguments:
- pair_rep: bfloat16 [320, 160, 128], P(('groups', 'row'), 'col'), parts along dimension 0, may hold values from -6 to 6
- residue_mask: int32 [320], P('groups'), parts along dimension 0, may hold values 0 or 1
- ln_gain: float32 [128], replicated, may hold values from 0.1 to 1.9
- left_proj: bfloat16 [128, 128], replicated, may hold values from -0.5 to 0.5
- left_gate: bfloat16 [128, 128], replicated, may hold values from -0.5 to 0.5
- right_proj: bfloat16 [128, 128], replicated, may hold values from -0.5 to 0.5
- right_gate: bfloat16 [128, 128], replicated, may hold values from -0.5 to 0.5
- hidden_gain: float32 [128], replicated, may hold values from 0.1 to 1.9
- out_proj: bfloat16 [128, 128], replicated, may hold values from -0.5 to 0.5
- out_gate: bfloat16 [128, 128], replicated, may hold values from -0.5 to 0.5
Outputs:
- update: bfloat16 [320, 160, 128], P(('groups', 'row'), ('col', 'chan')), parts along dimension 0
The draws below stay inside these ranges and needn't reach their ends.
There are 2 independent parts, one for each index of `groups`. The reference program is written for one: setup_inputs(seed, part) draws one part's arguments, and reference() takes and returns one part's arrays. A program takes and returns all parts, laid end to end along the dimension named above; an argument that names none is the same for every part. Nothing has to cross between parts.
All inputs are finite; a program needn't handle non-finite values.
Results may differ from the reference program's by a relative error of at most 0.015.
Values may be sent and summed in bfloat16 or wider, within the bound.
No kernel may reach another device: no remote copies, remote signals or barrier semaphores. Data moves between devices by JAX's collectives and lax.ppermute only.
A program may use at most 128 MiB of HBM per device.

```python
import jax
import jax.numpy as jnp
from jax import lax

C = 128
CH = 128
RES = 160


def touch_ends(array, key, low, high):
    dims = array.shape
    place = [jax.random.randint(jax.random.fold_in(key, axis), (), 0, dims[axis]) for axis in range(len(dims))]
    array = array.at[tuple(place)].set(low)
    longest = dims.index(max(dims))
    place[longest] = (place[longest] + 1) % dims[longest]
    return array.at[tuple(place)].set(high)


def block_levels(key, extent, shards, least, largest):
    loudness = 1.0
    for dim, blocks in shards:
        steps = jax.random.uniform(jax.random.fold_in(jax.random.fold_in(key, 6), dim), (blocks,), jnp.float32, least / len(shards), largest / len(shards))
        loudness = loudness * jnp.repeat(jnp.exp(steps), extent[dim] // blocks).reshape((-1,) + (1,) * (len(extent) - 1 - dim))
    return loudness


def gaussian(stream_key, dims, scale, bound, shards=(), held_as=jnp.bfloat16):
    entries = scale * jax.random.normal(stream_key, dims, jnp.float32)
    if shards:
        entries = entries * block_levels(stream_key, dims, shards, -0.22, 0.18)
    return jnp.clip(entries, -bound, bound).astype(held_as)


def setup_inputs(seed: int = 0, part: int = 0) -> dict:
    keys = jax.random.split(jax.random.key(seed), 11)
    part_splits = jax.random.split(jax.random.fold_in(keys[10], part), 11)
    pair_rep = gaussian(part_splits[0], (RES, RES, C), 1.0, 6.0, ((0, 8), (1, 2)))
    residue_mask = touch_ends((jax.random.randint(part_splits[1], (RES,), 0, 8) < 7).astype(jnp.int32), jax.random.fold_in(part_splits[1], 1), 0, 1)
    ln_gain = jnp.clip(1.0 + 0.18 * jax.random.normal(keys[2], (C,), jnp.float32), 0.1, 1.9)
    left_proj = gaussian(keys[3], (C, CH), C ** -0.5, 0.5)
    left_gate = gaussian(keys[4], (C, CH), C ** -0.5, 0.5)
    right_proj = gaussian(keys[5], (C, CH), C ** -0.5, 0.5)
    right_gate = gaussian(keys[6], (C, CH), C ** -0.5, 0.5)
    hidden_gain = jnp.clip(1.0 + 0.18 * jax.random.normal(keys[7], (CH,), jnp.float32), 0.1, 1.9)
    out_proj = gaussian(keys[8], (CH, C), CH ** -0.5, 0.5)
    out_gate = gaussian(keys[9], (C, C), C ** -0.5, 0.5)
    return {"pair_rep": pair_rep, "residue_mask": residue_mask, "ln_gain": ln_gain, "left_proj": left_proj, "left_gate": left_gate, "right_proj": right_proj, "right_gate": right_gate, "hidden_gain": hidden_gain, "out_proj": out_proj, "out_gate": out_gate}


def layer_norm(values, gain):
    center = lax.optimization_barrier(jnp.mean(values, axis=-1, keepdims=True))
    spread = lax.optimization_barrier(jnp.mean(jnp.square(values - center), axis=-1, keepdims=True))
    return (values - center) * lax.rsqrt(spread + 1e-05) * gain

def reference(pair_rep, residue_mask, ln_gain, left_proj, left_gate, right_proj, right_gate, hidden_gain, out_proj, out_gate):
    normed_pair = layer_norm(pair_rep.astype(jnp.float32), ln_gain).astype(jnp.bfloat16)
    flat_pair = normed_pair.reshape(RES * RES, C)
    mask_float = residue_mask.astype(jnp.float32)
    pair_mask = (mask_float[:, None] * mask_float[None, :])[:, :, None]

    def project(matrix):
        return jnp.dot(flat_pair, matrix, preferred_element_type=jnp.float32).reshape(RES, RES, -1)
    left_act = (pair_mask * jax.nn.sigmoid(project(left_gate)) * project(left_proj)).astype(jnp.bfloat16)
    right_act = (pair_mask * jax.nn.sigmoid(project(right_gate)) * project(right_proj)).astype(jnp.bfloat16)
    tri_sum = jnp.einsum('ikc,jkc->ijc', left_act.astype(jnp.float32), right_act.astype(jnp.float32), precision=lax.Precision.HIGHEST)
    normed_hidden = layer_norm(tri_sum, hidden_gain).astype(jnp.bfloat16)
    projected = jnp.dot(normed_hidden.reshape(RES * RES, CH), out_proj, preferred_element_type=jnp.float32).reshape(RES, RES, C)
    gating = jax.nn.sigmoid(project(out_gate))
    return (gating * projected).astype(jnp.bfloat16)
```

```python
import functools

import jax
import jax.numpy as jnp
from jax import lax
from jax.experimental import pallas as pl
from jax.experimental.pallas import tpu as pltpu
from jax.sharding import PartitionSpec as P

LINE = ("row", "col")
VMEM_LIMIT = 48 * 1024 * 1024


def layer_norm(values, gain):
    center = jnp.mean(values, axis=-1, keepdims=True)
    spread = jnp.mean(jnp.square(values - center), axis=-1, keepdims=True)
    return (values - center) * lax.rsqrt(spread + 1e-05) * gain


def gated_pair(normed_pair, matrices, pair_mask):
    tile_rows, tile_cols, pair_width = normed_pair.shape
    stacked = jnp.concatenate(matrices, axis=1)
    width = matrices[0].shape[1]
    projected = jnp.dot(
        normed_pair.reshape(tile_rows * tile_cols, pair_width),
        stacked,
        preferred_element_type=jnp.float32,
    )
    projected = projected.reshape(tile_rows, tile_cols, 4, width)
    masked = pair_mask[:, :, None]
    left_act = (masked * jax.nn.sigmoid(projected[:, :, 1]) * projected[:, :, 0]).astype(
        jnp.bfloat16
    )
    right_act = (masked * jax.nn.sigmoid(projected[:, :, 3]) * projected[:, :, 2]).astype(
        jnp.bfloat16
    )
    return (left_act, right_act)


def finish_output(normed_hidden, normed_pair, out_proj, out_gate):
    projected = jnp.einsum(
        "ijc,cd->ijd", normed_hidden, out_proj, preferred_element_type=jnp.float32
    )
    gating = jax.nn.sigmoid(
        jnp.einsum("ijc,cd->ijd", normed_pair, out_gate, preferred_element_type=jnp.float32)
    )
    return (gating * projected).astype(jnp.bfloat16)


def gathered(
    pair_rep,
    residue_mask,
    ln_gain,
    left_proj,
    left_gate,
    right_proj,
    right_gate,
    hidden_gain,
    out_proj,
    out_gate,
):
    tile_rows, tile_cols, pair_width = pair_rep.shape
    hidden_width = left_proj.shape[1]
    core_count = lax.axis_size("chan")
    core_index = lax.axis_index("chan")
    row_index = lax.axis_index("row")
    col_index = lax.axis_index("col")
    mask_float = residue_mask.astype(jnp.float32)
    row_mask = lax.dynamic_slice_in_dim(mask_float, row_index * tile_rows, tile_rows)
    core_cols = tile_cols // core_count
    matrices_all = (left_proj, left_gate, right_proj, right_gate)
    normed_pair = layer_norm(pair_rep.astype(jnp.float32), ln_gain).astype(jnp.bfloat16)
    col_mask = lax.dynamic_slice_in_dim(mask_float, col_index * tile_cols, tile_cols)
    pair_mask = row_mask[:, None] * col_mask[None, :]
    half_width = hidden_width // core_count
    matrices = tuple(
        (
            lax.dynamic_slice_in_dim(matrix, core_index * half_width, half_width, 1)
            for matrix in matrices_all
        )
    )
    left_act, right_act = gated_pair(normed_pair, matrices, pair_mask)
    partial_sums = jnp.einsum(
        "ikc,jkc->ijc",
        left_act,
        lax.all_gather(right_act, "row", axis=0, tiled=True),
        preferred_element_type=jnp.float32,
    )
    tri_sum = lax.psum_scatter(
        partial_sums.astype(jnp.bfloat16), "col", scatter_dimension=1, tiled=True
    ).astype(jnp.float32)
    full_hidden = lax.all_to_all(
        tri_sum.astype(jnp.bfloat16), "chan", split_axis=1, concat_axis=2, tiled=True
    ).astype(tri_sum.dtype)
    normed_hidden = layer_norm(full_hidden, hidden_gain).astype(jnp.bfloat16)
    own_pair = lax.dynamic_slice_in_dim(normed_pair, core_index * core_cols, core_cols, 1)
    return finish_output(normed_hidden, own_pair, out_proj, out_gate)


def whole(shape):
    return pl.BlockSpec(shape, lambda *_: (0,) * len(shape))


def normed_rows(pair_ref, gain_ref):
    rows, cols, width = pair_ref.shape
    values = pair_ref[...].astype(jnp.float32).reshape(rows * cols, width)
    return layer_norm(values, gain_ref[...]).astype(jnp.bfloat16)


def mask_block(mask_ref, flags_ref, rows, cols, width):
    first = flags_ref[0] * (rows * pl.num_programs(0)) + pl.program_id(0) * rows
    col_mask = jnp.zeros((1, cols), jnp.int32)
    for block in range(mask_ref.shape[1] // cols):
        part = mask_ref[:, block * cols : (block + 1) * cols]
        col_mask = jnp.where(flags_ref[1] == block, part, col_mask)
    spread = jnp.transpose(jnp.broadcast_to(col_mask.astype(jnp.float32), (width, cols)))
    lanes = lax.broadcasted_iota(jnp.int32, mask_ref.shape, 1)
    blocks = []
    for row in range(rows):
        present = jnp.sum(jnp.where(lanes == first + row, mask_ref[...], 0), axis=1, keepdims=True)
        blocks.append(spread * present.astype(jnp.float32))
    return jnp.concatenate(blocks, axis=0)


def right_kernel(flags_ref, pair_ref, mask_ref, gain_ref, proj_ref, gate_ref, right_ref):
    rows, cols, width = pair_ref.shape
    normed = normed_rows(pair_ref, gain_ref)
    masked = mask_block(mask_ref, flags_ref, rows, cols, width)
    stacked = jnp.concatenate([proj_ref[...], gate_ref[...]], axis=1)
    both = jnp.dot(normed, stacked, preferred_element_type=jnp.float32)
    act = masked * jax.nn.sigmoid(both[:, width:]) * both[:, :width]
    right_ref[...] = act.astype(jnp.bfloat16).reshape(rows, cols, width)


def left_kernel(
    flags_ref, pair_ref, mask_ref, gain_ref, proj_ref, gate_ref, out_gate_ref, left_ref, gating_ref
):
    rows, cols, width = pair_ref.shape
    normed = normed_rows(pair_ref, gain_ref)
    masked = mask_block(mask_ref, flags_ref, rows, cols, width)
    stacked = jnp.concatenate([proj_ref[...], gate_ref[...]], axis=1)
    both = jnp.dot(normed, stacked, preferred_element_type=jnp.float32)
    act = masked * jax.nn.sigmoid(both[:, width:]) * both[:, :width]
    left_ref[...] = act.astype(jnp.bfloat16).astype(jnp.float32)
    gating_ref[...] = jax.nn.sigmoid(
        jnp.dot(normed, out_gate_ref[...], preferred_element_type=jnp.float32)
    )


def triangle_kernel(rows, cols, flags_ref, left_ref, mine_ref, other_ref, sum_ref, held):
    width = held.shape[1]
    tile = rows * cols
    core = flags_ref[2]
    held[pl.ds(pl.multiple_of(core * tile, tile), tile), :] = (
        mine_ref[...].astype(jnp.float32).reshape(tile, width)
    )
    held[pl.ds(pl.multiple_of((1 - core) * tile, tile), tile), :] = (
        other_ref[...].astype(jnp.float32).reshape(tile, width)
    )
    group = 5

    def of_rows(block, _):
        def of_col(k, totals):
            right = held[pl.ds(k, 2 * rows, stride=cols), :]
            return tuple(
                totals[g] + left_ref[pl.ds((block * group + g) * cols + k, 1), :] * right
                for g in range(group)
            )

        start = tuple(jnp.zeros((2 * rows, width), jnp.float32) for _ in range(group))
        totals = lax.fori_loop(0, cols, of_col, start, unroll=8)
        for g in range(group):
            sum_ref[block * group + g] = totals[g].astype(jnp.bfloat16)
        return 0

    lax.fori_loop(0, rows // group, of_rows, 0)


def finish_kernel(
    flags_ref, near0, near1, far0, far1, gnear0, gnear1, gfar0, gfar1, gain_ref, proj_ref, gating_ref, out_ref
):
    rows, cols, width = out_ref.shape
    keeps_near, odd = flags_ref[3] == 1, flags_ref[4] == 1

    def total(a, b, c, d):
        f = lambda ref: ref[...].astype(jnp.float32)
        return jnp.where(keeps_near, f(a) + f(b), f(c) + f(d))

    first = total(near0, gnear0, far0, gfar0)
    second = total(near1, gnear1, far1, gfar1)
    hidden = jnp.concatenate(
        [jnp.where(odd, second, first), jnp.where(odd, first, second)], axis=1
    ).reshape(rows * cols, width)
    normed = layer_norm(hidden, gain_ref[...]).astype(jnp.bfloat16)
    projected = jnp.dot(normed, proj_ref[...], preferred_element_type=jnp.float32)
    out_ref[...] = (gating_ref[...] * projected).astype(jnp.bfloat16).reshape(rows, cols, width)


def call(kernel, micros, out_shape, in_specs, out_specs, grid, scratch=()):
    return pl.pallas_call(
        kernel,
        out_shape=out_shape,
        grid_spec=pltpu.PrefetchScalarGridSpec(
            num_scalar_prefetch=1,
            grid=grid,
            in_specs=in_specs,
            out_specs=out_specs,
            scratch_shapes=list(scratch),
        ),
        compiler_params=pltpu.CompilerParams(vmem_limit_bytes=VMEM_LIMIT),
        cost_estimate=pl.CostEstimate(
            flops=int(micros * 1.1e9), bytes_accessed=int(micros * 3e6), transcendentals=0
        ),
    )


def exchanged(
    pair_rep,
    residue_mask,
    ln_gain,
    left_proj,
    left_gate,
    right_proj,
    right_gate,
    hidden_gain,
    out_proj,
    out_gate,
):
    rows, cols, width = pair_rep.shape
    tile = rows * cols
    row = lax.axis_index("row")
    col = lax.axis_index("col")
    core = row % 2
    chip = row // 2
    keeps_near = (chip // 2 == col).astype(jnp.int32)
    flags = jnp.stack([row, col, core, keeps_near, chip % 2]).astype(jnp.int32)
    mask = residue_mask.reshape(1, -1)
    ln_gain = ln_gain.reshape(1, -1)
    hidden_gain = hidden_gain.reshape(1, -1)

    places = range(16)
    over_core = [(p, p ^ 2) for p in places]
    over_next = [(p, p ^ 4) for p in places]
    over_pair = [(p, p ^ 8) for p in places]
    near_sums = [(p, p ^ 1) for p in places if p // 8 != p % 2]
    far_sums = [(p, p ^ 1) for p in places if p // 8 == p % 2]
    send = lambda value, pairs: lax.ppermute(value, LINE, pairs)

    steps = 4
    block = rows // steps
    pair_spec = pl.BlockSpec((block, cols, width), lambda s, _: (s, 0, 0))
    flat_spec = pl.BlockSpec((block * cols, width), lambda s, _: (s, 0))
    square = whole((width, width))
    vector = whole((1, width))
    right = call(
        right_kernel,
        2.2,
        jax.ShapeDtypeStruct((rows, cols, width), jnp.bfloat16),
        [pair_spec, whole(mask.shape), vector, square, square],
        pair_spec,
        (steps,),
    )(flags, pair_rep, mask, ln_gain, right_proj, right_gate)

    from_pair = send(right, over_pair)
    from_next = send(right, over_next)
    from_core = send(right, over_core)

    left, gating = call(
        left_kernel,
        2.9,
        (
            jax.ShapeDtypeStruct((tile, width), jnp.float32),
            jax.ShapeDtypeStruct((tile, width), jnp.float32),
        ),
        [pair_spec, whole(mask.shape), vector, square, square, square],
        (flat_spec, flat_spec),
        (steps,),
    )(flags, pair_rep, mask, ln_gain, left_proj, left_gate, out_gate)

    tile_spec = whole((rows, cols, width))
    sums = call(
        functools.partial(triangle_kernel, rows, cols),
        4.2,
        jax.ShapeDtypeStruct((rows, 2 * rows, width), jnp.bfloat16),
        [whole((tile, width)), tile_spec, tile_spec],
        whole((rows, 2 * rows, width)),
        (1,),
        [pltpu.VMEM((2 * tile, width), jnp.float32)],
    )
    near0 = sums(flags, left, right, from_core)
    gnear0 = send(near0, near_sums)
    near1 = sums(flags, left, from_next, send(from_next, over_core))
    gnear1 = send(near1, near_sums)
    from_far = send(from_pair, over_next)
    far0 = sums(flags, left, from_pair, send(from_pair, over_core))
    gfar0 = send(far0, far_sums)
    far1 = sums(flags, left, from_far, send(from_far, over_core))
    gfar1 = send(far1, far_sums)

    part = whole((rows, 2 * rows, width))
    return call(
        finish_kernel,
        2.0,
        jax.ShapeDtypeStruct((rows, cols, width), jnp.bfloat16),
        [part] * 8 + [vector, square, whole((tile, width))],
        tile_spec,
        (1,),
    )(flags, near0, near1, far0, far1, gnear0, gnear1, gfar0, gfar1, hidden_gain, out_proj, gating)


def solution(mesh):
    in_specs = (
        P(("groups", "row"), "col", None),
        P("groups"),
        P(),
        P(),
        P(),
        P(),
        P(),
        P(),
        P(),
        P(),
    )
    out_specs = P(("groups", "row"), ("col", "chan"), None)
    short = mesh.shape["row"] == 8 and mesh.shape["col"] == 2 and mesh.shape["chan"] == 1
    local = exchanged if short else gathered
    return jax.shard_map(local, mesh=mesh, in_specs=in_specs, out_specs=out_specs, check_vma=False)
```

```python
import functools

import jax
import jax.numpy as jnp
from jax import lax
from jax.experimental import pallas as pl
from jax.experimental.pallas import tpu as pltpu
from jax.sharding import PartitionSpec as P

LINE = ("row", "col")
VMEM_LIMIT = 48 * 1024 * 1024
VECTOR_ROWS = 8
PAIR = 2
UNROLL = 10


def layer_norm(values, gain):
    center = jnp.mean(values, axis=-1, keepdims=True)
    spread = jnp.mean(jnp.square(values - center), axis=-1, keepdims=True)
    return (values - center) * lax.rsqrt(spread + 1e-05) * gain


def gated_pair(normed_pair, matrices, pair_mask):
    tile_rows, tile_cols, pair_width = normed_pair.shape
    stacked = jnp.concatenate(matrices, axis=1)
    width = matrices[0].shape[1]
    projected = jnp.dot(
        normed_pair.reshape(tile_rows * tile_cols, pair_width),
        stacked,
        preferred_element_type=jnp.float32,
    )
    projected = projected.reshape(tile_rows, tile_cols, 4, width)
    masked = pair_mask[:, :, None]
    left_act = (masked * jax.nn.sigmoid(projected[:, :, 1]) * projected[:, :, 0]).astype(
        jnp.bfloat16
    )
    right_act = (masked * jax.nn.sigmoid(projected[:, :, 3]) * projected[:, :, 2]).astype(
        jnp.bfloat16
    )
    return (left_act, right_act)


def finish_output(normed_hidden, normed_pair, out_proj, out_gate):
    projected = jnp.einsum(
        "ijc,cd->ijd", normed_hidden, out_proj, preferred_element_type=jnp.float32
    )
    gating = jax.nn.sigmoid(
        jnp.einsum("ijc,cd->ijd", normed_pair, out_gate, preferred_element_type=jnp.float32)
    )
    return (gating * projected).astype(jnp.bfloat16)


def gathered(
    pair_rep,
    residue_mask,
    ln_gain,
    left_proj,
    left_gate,
    right_proj,
    right_gate,
    hidden_gain,
    out_proj,
    out_gate,
):
    tile_rows, tile_cols, pair_width = pair_rep.shape
    hidden_width = left_proj.shape[1]
    core_count = lax.axis_size("chan")
    core_index = lax.axis_index("chan")
    row_index = lax.axis_index("row")
    col_index = lax.axis_index("col")
    mask_float = residue_mask.astype(jnp.float32)
    row_mask = lax.dynamic_slice_in_dim(mask_float, row_index * tile_rows, tile_rows)
    core_cols = tile_cols // core_count
    matrices_all = (left_proj, left_gate, right_proj, right_gate)
    normed_pair = layer_norm(pair_rep.astype(jnp.float32), ln_gain).astype(jnp.bfloat16)
    col_mask = lax.dynamic_slice_in_dim(mask_float, col_index * tile_cols, tile_cols)
    pair_mask = row_mask[:, None] * col_mask[None, :]
    half_width = hidden_width // core_count
    matrices = tuple(
        (
            lax.dynamic_slice_in_dim(matrix, core_index * half_width, half_width, 1)
            for matrix in matrices_all
        )
    )
    left_act, right_act = gated_pair(normed_pair, matrices, pair_mask)
    partial_sums = jnp.einsum(
        "ikc,jkc->ijc",
        left_act,
        lax.all_gather(right_act, "row", axis=0, tiled=True),
        preferred_element_type=jnp.float32,
    )
    tri_sum = lax.psum_scatter(
        partial_sums.astype(jnp.bfloat16), "col", scatter_dimension=1, tiled=True
    ).astype(jnp.float32)
    full_hidden = lax.all_to_all(
        tri_sum.astype(jnp.bfloat16), "chan", split_axis=1, concat_axis=2, tiled=True
    ).astype(tri_sum.dtype)
    normed_hidden = layer_norm(full_hidden, hidden_gain).astype(jnp.bfloat16)
    own_pair = lax.dynamic_slice_in_dim(normed_pair, core_index * core_cols, core_cols, 1)
    return finish_output(normed_hidden, own_pair, out_proj, out_gate)


def whole(shape):
    return pl.BlockSpec(shape, lambda *_: (0,) * len(shape))


def normed_rows(pair_ref, gain_ref):
    rows, cols, width = pair_ref.shape
    values = pair_ref[...].astype(jnp.float32).reshape(rows * cols, width)
    return layer_norm(values, gain_ref[...]).astype(jnp.bfloat16)


def mask_block(mask_ref, flags_ref, rows, cols, width):
    first = flags_ref[0] * (rows * pl.num_programs(0)) + pl.program_id(0) * rows
    col_mask = jnp.zeros((1, cols), jnp.int32)
    for block in range(mask_ref.shape[1] // cols):
        part = mask_ref[:, block * cols : (block + 1) * cols]
        col_mask = jnp.where(flags_ref[1] == block, part, col_mask)
    spread = jnp.transpose(jnp.broadcast_to(col_mask.astype(jnp.float32), (width, cols)))
    lanes = lax.broadcasted_iota(jnp.int32, mask_ref.shape, 1)
    blocks = []
    for row in range(rows):
        present = jnp.sum(jnp.where(lanes == first + row, mask_ref[...], 0), axis=1, keepdims=True)
        blocks.append(spread * present.astype(jnp.float32))
    return jnp.concatenate(blocks, axis=0)


def right_kernel(flags_ref, pair_ref, mask_ref, gain_ref, proj_ref, gate_ref, right_ref):
    rows, cols, width = pair_ref.shape
    normed = normed_rows(pair_ref, gain_ref)
    masked = mask_block(mask_ref, flags_ref, rows, cols, width)
    stacked = jnp.concatenate([proj_ref[...], gate_ref[...]], axis=1)
    both = jnp.dot(normed, stacked, preferred_element_type=jnp.float32)
    act = masked * jax.nn.sigmoid(both[:, width:]) * both[:, :width]
    right_ref[...] = act.astype(jnp.bfloat16).reshape(rows, cols, width)


def left_kernel(
    flags_ref,
    pair_ref,
    mask_ref,
    gain_ref,
    proj_ref,
    gate_ref,
    out_gate_ref,
    mine_ref,
    other_ref,
    left_ref,
    gating_ref,
    sum_ref,
    swap_ref,
    left_wide,
    right_wide,
):
    rows, cols, width = pair_ref.shape
    normed = normed_rows(pair_ref, gain_ref)
    masked = mask_block(mask_ref, flags_ref, rows, cols, width)
    stacked = jnp.concatenate([proj_ref[...], gate_ref[...]], axis=1)
    both = jnp.dot(normed, stacked, preferred_element_type=jnp.float32)
    act = masked * jax.nn.sigmoid(both[:, width:]) * both[:, :width]
    left_ref[...] = act.astype(jnp.bfloat16).reshape(rows, cols, width)
    gating_ref[...] = jax.nn.sigmoid(
        jnp.dot(normed, out_gate_ref[...], preferred_element_type=jnp.float32)
    )
    triangle([left_ref], [[mine_ref], [other_ref]], sum_ref, left_wide, right_wide)
    keeps_near = flags_ref[3] == 1

    @pl.when(keeps_near)
    def _():
        swap_ref[...] = left_ref[...]

    @pl.when(jnp.logical_not(keeps_near))
    def _():
        swap_ref[:, : 2 * rows] = sum_ref[...]
        swap_ref[:, 2 * rows :] = jnp.zeros((rows, cols - 2 * rows, width), jnp.bfloat16)


def run_sums(count, length):
    row = lax.broadcasted_iota(jnp.int32, (count, count * length), 0) * length
    col = lax.broadcasted_iota(jnp.int32, (count, count * length), 1)
    return jnp.where((col >= row) & (col < row + length), 1.0, 0.0).astype(jnp.bfloat16)


def triangle(lefts, tiles, sum_ref, left_wide, right_wide):
    rows, cols, width = lefts[0].shape
    size = rows * cols
    few = VECTOR_ROWS
    many = rows - few
    for b, left_ref in enumerate(lefts):
        left_wide[b * size : (b + 1) * size, :] = (
            left_ref[...].astype(jnp.float32).reshape(size, width)
        )
    held = few * cols
    blocks = [block for tile in tiles for block in tile]
    for n, block in enumerate(blocks):
        right_wide[n * held : (n + 1) * held, :] = (
            block[:few].astype(jnp.float32).reshape(held, width)
        )
    sum_many, sum_few = run_sums(many, cols), run_sums(few, 8)

    def of_rows(step, _):
        lines = [step * PAIR + n for n in range(PAIR)]
        narrow = [[left_ref[line] for line in lines] for left_ref in lefts]
        wide = [
            [
                left_wide[pl.ds(pl.multiple_of(b * size + line * cols, 8), cols), :].reshape(
                    cols // 8, 8, width
                )
                for line in lines
            ]
            for b in range(len(lefts))
        ]
        for t, tile in enumerate(tiles):
            last, partial = 0.0, [0.0] * PAIR
            for b, block in enumerate(tile):
                right = block[few:]
                products = jnp.concatenate(
                    [(right * left[None]).reshape(many * cols, width) for left in narrow[b]], axis=1
                )
                last = last + jnp.dot(sum_many, products, preferred_element_type=jnp.float32)
                n = t * len(tile) + b
                right = right_wide[n * held : (n + 1) * held, :]
                right = right.reshape(few, cols // 8, 8, width)
                partial = [
                    total + jnp.sum(right * left[None], axis=1).reshape(few * 8, width)
                    for total, left in zip(partial, wide[b])
                ]
            first = jnp.dot(
                sum_few,
                jnp.concatenate(partial, axis=1).astype(jnp.bfloat16),
                preferred_element_type=jnp.float32,
            )
            sums = jnp.concatenate([first, last], axis=0).astype(sum_ref.dtype)
            for n, line in enumerate(lines):
                sum_ref[line, t * rows : (t + 1) * rows, :] = sums[:, n * width : (n + 1) * width]
        return 0

    lax.fori_loop(0, rows // PAIR, of_rows, 0, unroll=UNROLL)


def middle_kernel(
    flags_ref,
    left_ref,
    next_mine,
    next_other,
    pair_mine,
    pair_other,
    kept_ref,
    sent_ref,
    both,
    left_wide,
    right_wide,
):
    keeps_near = flags_ref[3]
    triangle([left_ref], [[next_mine], [next_other]], both.at[1 - keeps_near], left_wide, right_wide)
    triangle([left_ref], [[pair_mine], [pair_other]], both.at[keeps_near], left_wide, right_wide)
    kept_ref[...] = both[0]
    sent_ref[...] = both[1]


def last_kernel(
    flags_ref, left_ref, given_ref, straight_ref, across_ref, sum_ref, left_wide, right_wide
):
    @pl.when(flags_ref[3] == 0)
    def _():
        triangle(
            [left_ref, given_ref], [[straight_ref, across_ref]], sum_ref, left_wide, right_wide
        )


def finish_kernel(
    flags_ref,
    left_ref,
    given_ref,
    straight_ref,
    across_ref,
    mine_ref,
    near_ref,
    kept_ref,
    kept_given_ref,
    gain_ref,
    proj_ref,
    gating_ref,
    out_ref,
    other_ref,
    left_wide,
    right_wide,
):
    last_kernel(
        flags_ref, left_ref, given_ref, straight_ref, across_ref, other_ref, left_wide, right_wide
    )
    rows, cols, width = out_ref.shape
    core, keeps_near, odd = flags_ref[2] == 1, flags_ref[3] == 1, flags_ref[4] == 1
    near = near_ref[...].astype(jnp.float32) + given_ref[:, : 2 * rows].astype(jnp.float32)
    far = jnp.concatenate([mine_ref[...], other_ref[...]], axis=1)
    swapped = kept_ref[...].astype(jnp.float32) + kept_given_ref[...].astype(jnp.float32)
    whole_near, next_near = keeps_near, jnp.logical_not(keeps_near)
    first = jnp.where(whole_near, near, swapped)
    second = jnp.where(next_near, far, swapped)
    parts = []
    for block in (jnp.where(odd, second, first), jnp.where(odd, first, second)):
        own, partner = block[:, :rows], block[:, rows:]
        parts += [jnp.where(core, partner, own), jnp.where(core, own, partner)]
    hidden = jnp.concatenate(parts, axis=1).reshape(rows * cols, width)
    normed = layer_norm(hidden, gain_ref[...]).astype(jnp.bfloat16)
    projected = jnp.dot(normed, proj_ref[...], preferred_element_type=jnp.float32)
    out_ref[...] = (gating_ref[...] * projected).astype(jnp.bfloat16).reshape(rows, cols, width)


def call(kernel, micros, out_shape, in_specs, out_specs, grid, scratch=()):
    return pl.pallas_call(
        kernel,
        out_shape=out_shape,
        grid_spec=pltpu.PrefetchScalarGridSpec(
            num_scalar_prefetch=1,
            grid=grid,
            in_specs=in_specs,
            out_specs=out_specs,
            scratch_shapes=list(scratch),
        ),
        compiler_params=pltpu.CompilerParams(vmem_limit_bytes=VMEM_LIMIT),
        cost_estimate=pl.CostEstimate(
            flops=int(micros * 1.1e9), bytes_accessed=int(micros * 3e6), transcendentals=0
        ),
    )


def exchanged(
    pair_rep,
    residue_mask,
    ln_gain,
    left_proj,
    left_gate,
    right_proj,
    right_gate,
    hidden_gain,
    out_proj,
    out_gate,
):
    rows, cols, width = pair_rep.shape
    tile = rows * cols
    row = lax.axis_index("row")
    col = lax.axis_index("col")
    core = row % 2
    chip = row // 2
    keeps_near = (chip // 2 == col).astype(jnp.int32)
    flags = jnp.stack([row, col, core, keeps_near, chip % 2]).astype(jnp.int32)
    mask = residue_mask.reshape(1, -1)
    ln_gain = ln_gain.reshape(1, -1)
    hidden_gain = hidden_gain.reshape(1, -1)

    places = range(16)
    over_core = [(p, p ^ 2) for p in places]
    over_next = [(p, p ^ 4) for p in places]
    over_pair = [(p, p ^ 8) for p in places]
    over_col = [(p, p ^ 1) for p in places]
    keeps_far = lambda p: p // 8 != p % 2
    straight = [(p, p ^ 4) for p in places if keeps_far(p ^ 4)]
    across = [(p, p ^ 5) for p in places if keeps_far(p ^ 5)]
    send = lambda value, pairs: lax.ppermute(value, LINE, pairs)

    steps = 4
    block = rows // steps
    pair_spec = pl.BlockSpec((block, cols, width), lambda s, _: (s, 0, 0))
    square = whole((width, width))
    vector = whole((1, width))
    right = call(
        right_kernel,
        2.2,
        jax.ShapeDtypeStruct((rows, cols, width), jnp.bfloat16),
        [pair_spec, whole(mask.shape), vector, square, square],
        pair_spec,
        (steps,),
    )(flags, pair_rep, mask, ln_gain, right_proj, right_gate)

    from_pair = send(right, over_pair)
    from_next = send(right, over_next)
    from_core = send(right, over_core)

    after = lambda value, *last: lax.optimization_barrier((value, *last))[0]
    bf16 = lambda *shape: jax.ShapeDtypeStruct(shape, jnp.bfloat16)
    f32 = lambda *shape: jax.ShapeDtypeStruct(shape, jnp.float32)
    tile_spec = whole((rows, cols, width))
    flat_spec = whole((tile, width))
    two, one = (rows, 2 * rows, width), (rows, rows, width)
    held = VECTOR_ROWS * cols
    wide = lambda lefts, blocks: [
        pltpu.VMEM((lefts * tile, width), jnp.float32),
        pltpu.VMEM((blocks * held, width), jnp.float32),
    ]
    left, gating, near, swap = call(
        left_kernel,
        4.0,
        (bf16(rows, cols, width), f32(tile, width), bf16(*two), bf16(rows, cols, width)),
        [tile_spec, whole(mask.shape), vector, square, square, square, tile_spec, tile_spec],
        (tile_spec, flat_spec, whole(two), tile_spec),
        (1,),
        wide(1, 2),
    )(flags, pair_rep, mask, ln_gain, left_proj, left_gate, out_gate, right, from_core)
    given = send(swap, over_col)

    from_pair = after(from_pair, left)
    from_next = after(from_next, from_pair, given)
    far_straight, far_across = send(from_pair, straight), send(from_pair, across)
    kept, sent = call(
        middle_kernel,
        5.7,
        (bf16(*two), bf16(*two)),
        [tile_spec] * 5,
        (whole(two), whole(two)),
        (1,),
        [pltpu.VMEM((2, *two), jnp.bfloat16)] + wide(1, 2),
    )(flags, left, from_next, send(from_next, over_core), from_pair, send(from_pair, over_core))
    kept_given = send(sent, over_col)

    far_straight, far_across = after(far_straight, sent), after(far_across, sent)
    other_straight, other_across = send(far_straight, over_core), send(far_across, over_core)
    mine = call(
        last_kernel, 2.9, f32(*one), [tile_spec] * 4, whole(one), (1,), wide(2, 2)
    )(flags, left, given, far_straight, far_across)
    return call(
        finish_kernel,
        5.0,
        bf16(rows, cols, width),
        [tile_spec] * 4 + [whole(one)] + [whole(two)] * 3 + [vector, square, flat_spec],
        tile_spec,
        (1,),
        [pltpu.VMEM(one, jnp.float32)] + wide(2, 2),
    )(
        flags,
        left,
        given,
        other_straight,
        other_across,
        mine,
        near,
        kept,
        kept_given,
        hidden_gain,
        out_proj,
        gating,
    )


def solution(mesh):
    in_specs = (
        P(("groups", "row"), "col", None),
        P("groups"),
        P(),
        P(),
        P(),
        P(),
        P(),
        P(),
        P(),
        P(),
    )
    out_specs = P(("groups", "row"), ("col", "chan"), None)
    short = mesh.shape["row"] == 8 and mesh.shape["col"] == 2 and mesh.shape["chan"] == 1
    local = exchanged if short else gathered
    return jax.shard_map(local, mesh=mesh, in_specs=in_specs, out_specs=out_specs, check_vma=False)
```

```python
import functools

import jax
import jax.numpy as jnp
from jax import lax
from jax.experimental import pallas as pl
from jax.experimental.pallas import tpu as pltpu
from jax.sharding import PartitionSpec as P

LINE = ("row", "col")
VMEM_LIMIT = 48 * 1024 * 1024
VECTOR_ROWS = 8
PAIR = 2
UNROLL = 10


def layer_norm(values, gain):
    center = jnp.mean(values, axis=-1, keepdims=True)
    spread = jnp.mean(jnp.square(values - center), axis=-1, keepdims=True)
    return (values - center) * lax.rsqrt(spread + 1e-05) * gain


def gated_pair(normed_pair, matrices, pair_mask):
    tile_rows, tile_cols, pair_width = normed_pair.shape
    stacked = jnp.concatenate(matrices, axis=1)
    width = matrices[0].shape[1]
    projected = jnp.dot(
        normed_pair.reshape(tile_rows * tile_cols, pair_width),
        stacked,
        preferred_element_type=jnp.float32,
    )
    projected = projected.reshape(tile_rows, tile_cols, 4, width)
    masked = pair_mask[:, :, None]
    left_act = (masked * jax.nn.sigmoid(projected[:, :, 1]) * projected[:, :, 0]).astype(
        jnp.bfloat16
    )
    right_act = (masked * jax.nn.sigmoid(projected[:, :, 3]) * projected[:, :, 2]).astype(
        jnp.bfloat16
    )
    return (left_act, right_act)


def finish_output(normed_hidden, normed_pair, out_proj, out_gate):
    projected = jnp.einsum(
        "ijc,cd->ijd", normed_hidden, out_proj, preferred_element_type=jnp.float32
    )
    gating = jax.nn.sigmoid(
        jnp.einsum("ijc,cd->ijd", normed_pair, out_gate, preferred_element_type=jnp.float32)
    )
    return (gating * projected).astype(jnp.bfloat16)


def gathered(
    pair_rep,
    residue_mask,
    ln_gain,
    left_proj,
    left_gate,
    right_proj,
    right_gate,
    hidden_gain,
    out_proj,
    out_gate,
):
    tile_rows, tile_cols, pair_width = pair_rep.shape
    hidden_width = left_proj.shape[1]
    core_count = lax.axis_size("chan")
    core_index = lax.axis_index("chan")
    row_index = lax.axis_index("row")
    col_index = lax.axis_index("col")
    mask_float = residue_mask.astype(jnp.float32)
    row_mask = lax.dynamic_slice_in_dim(mask_float, row_index * tile_rows, tile_rows)
    core_cols = tile_cols // core_count
    matrices_all = (left_proj, left_gate, right_proj, right_gate)
    normed_pair = layer_norm(pair_rep.astype(jnp.float32), ln_gain).astype(jnp.bfloat16)
    col_mask = lax.dynamic_slice_in_dim(mask_float, col_index * tile_cols, tile_cols)
    pair_mask = row_mask[:, None] * col_mask[None, :]
    half_width = hidden_width // core_count
    matrices = tuple(
        (
            lax.dynamic_slice_in_dim(matrix, core_index * half_width, half_width, 1)
            for matrix in matrices_all
        )
    )
    left_act, right_act = gated_pair(normed_pair, matrices, pair_mask)
    partial_sums = jnp.einsum(
        "ikc,jkc->ijc",
        left_act,
        lax.all_gather(right_act, "row", axis=0, tiled=True),
        preferred_element_type=jnp.float32,
    )
    tri_sum = lax.psum_scatter(
        partial_sums.astype(jnp.bfloat16), "col", scatter_dimension=1, tiled=True
    ).astype(jnp.float32)
    full_hidden = lax.all_to_all(
        tri_sum.astype(jnp.bfloat16), "chan", split_axis=1, concat_axis=2, tiled=True
    ).astype(tri_sum.dtype)
    normed_hidden = layer_norm(full_hidden, hidden_gain).astype(jnp.bfloat16)
    own_pair = lax.dynamic_slice_in_dim(normed_pair, core_index * core_cols, core_cols, 1)
    return finish_output(normed_hidden, own_pair, out_proj, out_gate)


def whole(shape):
    return pl.BlockSpec(shape, lambda *_: (0,) * len(shape))


def normed_rows(pair_ref, gain_ref):
    rows, cols, width = pair_ref.shape
    values = pair_ref[...].astype(jnp.float32).reshape(rows * cols, width)
    return layer_norm(values, gain_ref[...]).astype(jnp.bfloat16)


def mask_block(mask_ref, flags_ref, rows, cols, width):
    first = flags_ref[0] * (rows * pl.num_programs(0)) + pl.program_id(0) * rows
    col_mask = jnp.zeros((1, cols), jnp.int32)
    for block in range(mask_ref.shape[1] // cols):
        part = mask_ref[:, block * cols : (block + 1) * cols]
        col_mask = jnp.where(flags_ref[1] == block, part, col_mask)
    spread = jnp.transpose(jnp.broadcast_to(col_mask.astype(jnp.float32), (width, cols)))
    lanes = lax.broadcasted_iota(jnp.int32, mask_ref.shape, 1)
    blocks = []
    for row in range(rows):
        present = jnp.sum(jnp.where(lanes == first + row, mask_ref[...], 0), axis=1, keepdims=True)
        blocks.append(spread * present.astype(jnp.float32))
    return jnp.concatenate(blocks, axis=0)


def right_kernel(flags_ref, pair_ref, mask_ref, gain_ref, proj_ref, gate_ref, right_ref):
    rows, cols, width = pair_ref.shape
    normed = normed_rows(pair_ref, gain_ref)
    masked = mask_block(mask_ref, flags_ref, rows, cols, width)
    stacked = jnp.concatenate([proj_ref[...], gate_ref[...]], axis=1)
    both = jnp.dot(normed, stacked, preferred_element_type=jnp.float32)
    act = masked * jax.nn.sigmoid(both[:, width:]) * both[:, :width]
    right_ref[...] = act.astype(jnp.bfloat16).reshape(rows, cols, width)


def left_kernel(
    flags_ref,
    pair_ref,
    mask_ref,
    gain_ref,
    proj_ref,
    gate_ref,
    out_gate_ref,
    mine_ref,
    other_ref,
    left_ref,
    gating_ref,
    sum_ref,
    swap_ref,
    left_wide,
    right_wide,
):
    rows, cols, width = pair_ref.shape
    normed = normed_rows(pair_ref, gain_ref)
    masked = mask_block(mask_ref, flags_ref, rows, cols, width)
    stacked = jnp.concatenate([proj_ref[...], gate_ref[...]], axis=1)
    both = jnp.dot(normed, stacked, preferred_element_type=jnp.float32)
    act = masked * jax.nn.sigmoid(both[:, width:]) * both[:, :width]
    left_ref[...] = act.astype(jnp.bfloat16).reshape(rows, cols, width)
    gating_ref[...] = jax.nn.sigmoid(
        jnp.dot(normed, out_gate_ref[...], preferred_element_type=jnp.float32)
    )
    triangle([left_ref], [[mine_ref], [other_ref]], sum_ref, left_wide, right_wide)
    keeps_near = flags_ref[3] == 1

    @pl.when(keeps_near)
    def _():
        swap_ref[...] = left_ref[...]

    @pl.when(jnp.logical_not(keeps_near))
    def _():
        swap_ref[:, : 2 * rows] = sum_ref[...]
        swap_ref[:, 2 * rows :] = jnp.zeros((rows, cols - 2 * rows, width), jnp.bfloat16)


def run_sums(count, length):
    row = lax.broadcasted_iota(jnp.int32, (count, count * length), 0) * length
    col = lax.broadcasted_iota(jnp.int32, (count, count * length), 1)
    return jnp.where((col >= row) & (col < row + length), 1.0, 0.0).astype(jnp.bfloat16)


def triangle(lefts, tiles, sum_ref, left_wide, right_wide):
    rows, cols, width = lefts[0].shape
    size = rows * cols
    few = VECTOR_ROWS
    many = rows - few
    for b, left_ref in enumerate(lefts):
        left_wide[b * size : (b + 1) * size, :] = (
            left_ref[...].astype(jnp.float32).reshape(size, width)
        )
    held = few * cols
    blocks = [block for tile in tiles for block in tile]
    for n, block in enumerate(blocks):
        right_wide[n * held : (n + 1) * held, :] = (
            block[:few].astype(jnp.float32).reshape(held, width)
        )
    sum_many, sum_few = run_sums(many, cols), run_sums(few, 8)

    def of_rows(step, _):
        lines = [step * PAIR + n for n in range(PAIR)]
        narrow = [[left_ref[line] for line in lines] for left_ref in lefts]
        wide = [
            [
                left_wide[pl.ds(pl.multiple_of(b * size + line * cols, 8), cols), :].reshape(
                    cols // 8, 8, width
                )
                for line in lines
            ]
            for b in range(len(lefts))
        ]
        for t, tile in enumerate(tiles):
            last, partial = 0.0, [0.0] * PAIR
            for b, block in enumerate(tile):
                right = block[few:]
                products = jnp.concatenate(
                    [(right * left[None]).reshape(many * cols, width) for left in narrow[b]], axis=1
                )
                last = last + jnp.dot(sum_many, products, preferred_element_type=jnp.float32)
                n = t * len(tile) + b
                right = right_wide[n * held : (n + 1) * held, :]
                right = right.reshape(few, cols // 8, 8, width)
                partial = [
                    total + jnp.sum(right * left[None], axis=1).reshape(few * 8, width)
                    for total, left in zip(partial, wide[b])
                ]
            first = jnp.dot(
                sum_few,
                jnp.concatenate(partial, axis=1).astype(jnp.bfloat16),
                preferred_element_type=jnp.float32,
            )
            sums = jnp.concatenate([first, last], axis=0).astype(sum_ref.dtype)
            for n, line in enumerate(lines):
                sum_ref[line, t * rows : (t + 1) * rows, :] = sums[:, n * width : (n + 1) * width]
        return 0

    lax.fori_loop(0, rows // PAIR, of_rows, 0, unroll=UNROLL)


def middle_kernel(
    flags_ref,
    left_ref,
    left_other,
    next_ref,
    pair_ref,
    kept_own,
    kept_other,
    sent_own,
    sent_other,
    both,
    left_wide,
    right_wide,
):
    rows = left_ref.shape[0]
    keeps_near = flags_ref[3] == 1
    for left, kept, sent in ((left_ref, kept_own, sent_own), (left_other, kept_other, sent_other)):
        triangle([left], [[next_ref], [pair_ref]], both, left_wide, right_wide)
        of_next, of_pair = both[:, :rows], both[:, rows:]
        kept[...] = jnp.where(keeps_near, of_next, of_pair).astype(jnp.bfloat16)
        sent[...] = jnp.where(keeps_near, of_pair, of_next).astype(jnp.bfloat16)


def last_kernel(
    flags_ref, left_ref, given_ref, straight_ref, across_ref, sum_ref, left_wide, right_wide
):
    @pl.when(flags_ref[3] == 0)
    def _():
        triangle(
            [left_ref, given_ref], [[straight_ref, across_ref]], sum_ref, left_wide, right_wide
        )


def finished(flags_ref, own, partner, at, gain_ref, proj_ref, gating_ref):
    rows, _, width = own.shape
    core = flags_ref[2] == 1
    hidden = jnp.concatenate(
        [jnp.where(core, partner, own), jnp.where(core, own, partner)], axis=1
    ).reshape(2 * rows * rows, width)
    normed = layer_norm(hidden, gain_ref[...]).astype(jnp.bfloat16)
    projected = jnp.dot(normed, proj_ref[...], preferred_element_type=jnp.float32)
    gating = jnp.where(at == 1, gating_ref[:, 2 * rows :], gating_ref[:, : 2 * rows])
    return gating * projected.reshape(rows, 2 * rows, width)


def swapped_kernel(
    flags_ref,
    own_ref,
    own_given,
    partner_ref,
    partner_given,
    gain_ref,
    proj_ref,
    gating_ref,
    out_ref,
):
    keeps_near, odd = flags_ref[3], flags_ref[4]
    total = lambda a, b: a[...].astype(jnp.float32) + b[...].astype(jnp.float32)
    at = jnp.where(keeps_near == 1, 1 - odd, odd)
    out_ref[...] = finished(
        flags_ref,
        total(own_ref, own_given),
        total(partner_ref, partner_given),
        at,
        gain_ref,
        proj_ref,
        gating_ref,
    ).astype(jnp.bfloat16)


def finish_kernel(
    flags_ref,
    left_ref,
    given_ref,
    straight_ref,
    across_ref,
    mine_ref,
    near_ref,
    done_ref,
    gain_ref,
    proj_ref,
    gating_ref,
    out_ref,
    other_ref,
    left_wide,
    right_wide,
):
    last_kernel(
        flags_ref, left_ref, given_ref, straight_ref, across_ref, other_ref, left_wide, right_wide
    )
    rows = out_ref.shape[0]
    keeps_near, odd = flags_ref[3] == 1, flags_ref[4]
    near = near_ref[...].astype(jnp.float32) + given_ref[:, : 2 * rows].astype(jnp.float32)
    own = jnp.where(keeps_near, near[:, :rows], mine_ref[...])
    partner = jnp.where(keeps_near, near[:, rows:], other_ref[...])
    at = jnp.where(keeps_near, odd, 1 - odd)
    result = finished(flags_ref, own, partner, at, gain_ref, proj_ref, gating_ref)
    done = done_ref[...].astype(jnp.float32)
    out_ref[...] = jnp.concatenate(
        [jnp.where(at == 1, done, result), jnp.where(at == 1, result, done)], axis=1
    ).astype(jnp.bfloat16)


def call(kernel, micros, out_shape, in_specs, out_specs, grid, scratch=()):
    return pl.pallas_call(
        kernel,
        out_shape=out_shape,
        grid_spec=pltpu.PrefetchScalarGridSpec(
            num_scalar_prefetch=1,
            grid=grid,
            in_specs=in_specs,
            out_specs=out_specs,
            scratch_shapes=list(scratch),
        ),
        compiler_params=pltpu.CompilerParams(vmem_limit_bytes=VMEM_LIMIT),
        cost_estimate=pl.CostEstimate(
            flops=int(micros * 1.1e9), bytes_accessed=int(micros * 3e6), transcendentals=0
        ),
    )


def exchanged(
    pair_rep,
    residue_mask,
    ln_gain,
    left_proj,
    left_gate,
    right_proj,
    right_gate,
    hidden_gain,
    out_proj,
    out_gate,
):
    rows, cols, width = pair_rep.shape
    tile = rows * cols
    row = lax.axis_index("row")
    col = lax.axis_index("col")
    core = row % 2
    chip = row // 2
    keeps_near = (chip // 2 == col).astype(jnp.int32)
    flags = jnp.stack([row, col, core, keeps_near, chip % 2]).astype(jnp.int32)
    mask = residue_mask.reshape(1, -1)
    ln_gain = ln_gain.reshape(1, -1)
    hidden_gain = hidden_gain.reshape(1, -1)

    places = range(16)
    over_core = [(p, p ^ 2) for p in places]
    over_next = [(p, p ^ 4) for p in places]
    over_pair = [(p, p ^ 8) for p in places]
    over_col = [(p, p ^ 1) for p in places]
    over_both = [(p, p ^ 3) for p in places]
    keeps_far = lambda p: p // 8 != p % 2
    straight = [(p, p ^ 4) for p in places if keeps_far(p ^ 4)]
    across = [(p, p ^ 5) for p in places if keeps_far(p ^ 5)]
    send = lambda value, pairs: lax.ppermute(value, LINE, pairs)

    steps = 4
    block = rows // steps
    pair_spec = pl.BlockSpec((block, cols, width), lambda s, _: (s, 0, 0))
    square = whole((width, width))
    vector = whole((1, width))
    right = call(
        right_kernel,
        2.2,
        jax.ShapeDtypeStruct((rows, cols, width), jnp.bfloat16),
        [pair_spec, whole(mask.shape), vector, square, square],
        pair_spec,
        (steps,),
    )(flags, pair_rep, mask, ln_gain, right_proj, right_gate)

    from_pair = send(right, over_pair)
    from_next = send(right, over_next)
    from_core = send(right, over_core)

    after = lambda value, *last: lax.optimization_barrier((value, *last))[0]
    bf16 = lambda *shape: jax.ShapeDtypeStruct(shape, jnp.bfloat16)
    f32 = lambda *shape: jax.ShapeDtypeStruct(shape, jnp.float32)
    tile_spec = whole((rows, cols, width))
    flat_spec = whole((tile, width))
    two, one = (rows, 2 * rows, width), (rows, rows, width)
    held = VECTOR_ROWS * cols
    wide = lambda lefts, blocks: [
        pltpu.VMEM((lefts * tile, width), jnp.float32),
        pltpu.VMEM((blocks * held, width), jnp.float32),
    ]
    left, gating, near, swap = call(
        left_kernel,
        4.0,
        (bf16(rows, cols, width), f32(tile, width), bf16(*two), bf16(rows, cols, width)),
        [tile_spec, whole(mask.shape), vector, square, square, square, tile_spec, tile_spec],
        (tile_spec, flat_spec, whole(two), tile_spec),
        (1,),
        wide(1, 2),
    )(flags, pair_rep, mask, ln_gain, left_proj, left_gate, out_gate, right, from_core)
    given = send(swap, over_col)
    left_other = send(left, over_core)

    from_pair = after(from_pair, left)
    from_next = after(from_next, from_pair, given)
    far_straight, far_across = send(from_pair, straight), send(from_pair, across)
    kept_own, kept_other, sent_own, sent_other = call(
        middle_kernel,
        5.7,
        (bf16(*one),) * 4,
        [tile_spec] * 4,
        (whole(one),) * 4,
        (1,),
        [pltpu.VMEM(two, jnp.float32)] + wide(1, 2),
    )(flags, left, after(left_other, from_pair), from_next, from_pair)
    kept_given = send(sent_own, over_col)
    partner_given = send(sent_other, over_both)
    partner = send(kept_other, over_core)

    far_straight, far_across = after(far_straight, kept_own), after(far_across, kept_own)
    other_straight, other_across = send(far_straight, over_core), send(far_across, over_core)
    mine = call(
        last_kernel, 0.1, f32(*one), [tile_spec] * 4, whole(one), (1,), wide(2, 2)
    )(flags, left, given, far_straight, far_across)
    gating = gating.reshape(rows, cols, width)
    done = call(
        swapped_kernel,
        8.0,
        bf16(*two),
        [whole(one)] * 4 + [vector, square, tile_spec],
        whole(two),
        (1,),
    )(flags, kept_own, kept_given, partner, partner_given, hidden_gain, out_proj, gating)
    other_straight, other_across = after(other_straight, done), after(other_across, done)
    return call(
        finish_kernel,
        4.0,
        bf16(rows, cols, width),
        [tile_spec] * 4 + [whole(one), whole(two), whole(two), vector, square, tile_spec],
        tile_spec,
        (1,),
        [pltpu.VMEM(one, jnp.float32)] + wide(2, 2),
    )(
        flags,
        left,
        given,
        other_straight,
        other_across,
        mine,
        near,
        done,
        hidden_gain,
        out_proj,
        gating,
    )


def solution(mesh):
    in_specs = (
        P(("groups", "row"), "col", None),
        P("groups"),
        P(),
        P(),
        P(),
        P(),
        P(),
        P(),
        P(),
        P(),
    )
    out_specs = P(("groups", "row"), ("col", "chan"), None)
    short = mesh.shape["row"] == 8 and mesh.shape["col"] == 2 and mesh.shape["chan"] == 1
    local = exchanged if short else gathered
    return jax.shard_map(local, mesh=mesh, in_specs=in_specs, out_specs=out_specs, check_vma=False)
```

```python
import functools

import jax
import jax.numpy as jnp
from jax import lax
from jax.experimental import pallas as pl
from jax.experimental.pallas import tpu as pltpu
from jax.sharding import PartitionSpec as P

LINE = ("row", "col")
VMEM_LIMIT = 48 * 1024 * 1024
VECTOR_ROWS = 16
PAIR = 2
UNROLL = 10


def layer_norm(values, gain):
    center = jnp.mean(values, axis=-1, keepdims=True)
    spread = jnp.mean(jnp.square(values - center), axis=-1, keepdims=True)
    return (values - center) * lax.rsqrt(spread + 1e-05) * gain


def gated_pair(normed_pair, matrices, pair_mask):
    tile_rows, tile_cols, pair_width = normed_pair.shape
    stacked = jnp.concatenate(matrices, axis=1)
    width = matrices[0].shape[1]
    projected = jnp.dot(
        normed_pair.reshape(tile_rows * tile_cols, pair_width),
        stacked,
        preferred_element_type=jnp.float32,
    )
    projected = projected.reshape(tile_rows, tile_cols, 4, width)
    masked = pair_mask[:, :, None]
    left_act = (masked * jax.nn.sigmoid(projected[:, :, 1]) * projected[:, :, 0]).astype(
        jnp.bfloat16
    )
    right_act = (masked * jax.nn.sigmoid(projected[:, :, 3]) * projected[:, :, 2]).astype(
        jnp.bfloat16
    )
    return (left_act, right_act)


def finish_output(normed_hidden, normed_pair, out_proj, out_gate):
    projected = jnp.einsum(
        "ijc,cd->ijd", normed_hidden, out_proj, preferred_element_type=jnp.float32
    )
    gating = jax.nn.sigmoid(
        jnp.einsum("ijc,cd->ijd", normed_pair, out_gate, preferred_element_type=jnp.float32)
    )
    return (gating * projected).astype(jnp.bfloat16)


def gathered(
    pair_rep,
    residue_mask,
    ln_gain,
    left_proj,
    left_gate,
    right_proj,
    right_gate,
    hidden_gain,
    out_proj,
    out_gate,
):
    tile_rows, tile_cols, pair_width = pair_rep.shape
    hidden_width = left_proj.shape[1]
    core_count = lax.axis_size("chan")
    core_index = lax.axis_index("chan")
    row_index = lax.axis_index("row")
    col_index = lax.axis_index("col")
    mask_float = residue_mask.astype(jnp.float32)
    row_mask = lax.dynamic_slice_in_dim(mask_float, row_index * tile_rows, tile_rows)
    core_cols = tile_cols // core_count
    matrices_all = (left_proj, left_gate, right_proj, right_gate)
    normed_pair = layer_norm(pair_rep.astype(jnp.float32), ln_gain).astype(jnp.bfloat16)
    col_mask = lax.dynamic_slice_in_dim(mask_float, col_index * tile_cols, tile_cols)
    pair_mask = row_mask[:, None] * col_mask[None, :]
    half_width = hidden_width // core_count
    matrices = tuple(
        (
            lax.dynamic_slice_in_dim(matrix, core_index * half_width, half_width, 1)
            for matrix in matrices_all
        )
    )
    left_act, right_act = gated_pair(normed_pair, matrices, pair_mask)
    partial_sums = jnp.einsum(
        "ikc,jkc->ijc",
        left_act,
        lax.all_gather(right_act, "row", axis=0, tiled=True),
        preferred_element_type=jnp.float32,
    )
    tri_sum = lax.psum_scatter(
        partial_sums.astype(jnp.bfloat16), "col", scatter_dimension=1, tiled=True
    ).astype(jnp.float32)
    full_hidden = lax.all_to_all(
        tri_sum.astype(jnp.bfloat16), "chan", split_axis=1, concat_axis=2, tiled=True
    ).astype(tri_sum.dtype)
    normed_hidden = layer_norm(full_hidden, hidden_gain).astype(jnp.bfloat16)
    own_pair = lax.dynamic_slice_in_dim(normed_pair, core_index * core_cols, core_cols, 1)
    return finish_output(normed_hidden, own_pair, out_proj, out_gate)


def normed_rows(pair_ref, gain_ref):
    rows, cols, width = pair_ref.shape
    values = pair_ref[...].astype(jnp.float32).reshape(rows * cols, width)
    return layer_norm(values, gain_ref[...]).astype(jnp.bfloat16)


def mask_block(mask_ref, flags_ref, rows, cols, width):
    first = flags_ref[0] * rows
    col_mask = jnp.zeros((1, cols), jnp.int32)
    for block in range(mask_ref.shape[1] // cols):
        part = mask_ref[:, block * cols : (block + 1) * cols]
        col_mask = jnp.where(flags_ref[1] == block, part, col_mask)
    spread = jnp.transpose(jnp.broadcast_to(col_mask.astype(jnp.float32), (width, cols)))
    lanes = lax.broadcasted_iota(jnp.int32, mask_ref.shape, 1)
    blocks = []
    for row in range(rows):
        present = jnp.sum(jnp.where(lanes == first + row, mask_ref[...], 0), axis=1, keepdims=True)
        blocks.append(spread * present.astype(jnp.float32))
    return jnp.concatenate(blocks, axis=0)


def right_kernel(flags_ref, pair_ref, mask_ref, gain_ref, proj_ref, gate_ref, right_ref):
    rows, cols, width = pair_ref.shape
    normed = normed_rows(pair_ref, gain_ref)
    masked = mask_block(mask_ref, flags_ref, rows, cols, width)
    stacked = jnp.concatenate([proj_ref[...], gate_ref[...]], axis=1)
    both = jnp.dot(normed, stacked, preferred_element_type=jnp.float32)
    act = masked * jax.nn.sigmoid(both[:, width:]) * both[:, :width]
    right_ref[...] = act.astype(jnp.bfloat16).reshape(rows, cols, width)


def left_kernel(
    flags_ref,
    pair_ref,
    mask_ref,
    gain_ref,
    proj_ref,
    gate_ref,
    out_gate_ref,
    mine_ref,
    other_ref,
    hidden_gain_ref,
    left_ref,
    gating_ref,
    sum_ref,
    swap_ref,
    held_gain_ref,
    right_wide,
):
    rows, cols, width = pair_ref.shape
    normed = normed_rows(pair_ref, gain_ref)
    masked = mask_block(mask_ref, flags_ref, rows, cols, width)
    stacked = jnp.concatenate([proj_ref[...], gate_ref[...]], axis=1)
    both = jnp.dot(normed, stacked, preferred_element_type=jnp.float32)
    act = masked * jax.nn.sigmoid(both[:, width:]) * both[:, :width]
    left_ref[...] = act.astype(jnp.bfloat16).reshape(rows, cols, width)
    gating_ref[...] = jax.nn.sigmoid(
        jnp.dot(normed, out_gate_ref[...], preferred_element_type=jnp.float32)
    )
    triangle(left_ref, [mine_ref, other_ref], sum_ref, right_wide)
    held_gain_ref[...] = hidden_gain_ref[...]
    keeps_near = flags_ref[3] == 1

    @pl.when(keeps_near)
    def _():
        swap_ref[...] = left_ref[...]

    @pl.when(jnp.logical_not(keeps_near))
    def _():
        swap_ref[:, : 2 * rows] = sum_ref[...]
        swap_ref[:, 2 * rows :] = jnp.zeros((rows, cols - 2 * rows, width), jnp.bfloat16)


def run_sums(count, length):
    row = lax.broadcasted_iota(jnp.int32, (count, count * length), 0) * length
    col = lax.broadcasted_iota(jnp.int32, (count, count * length), 1)
    return jnp.where((col >= row) & (col < row + length), 1.0, 0.0).astype(jnp.bfloat16)


def triangle(left_ref, tiles, sum_ref, right_wide, more=False):
    rows, cols, width = left_ref.shape
    few = VECTOR_ROWS
    many = rows - few
    for t, tile in enumerate(tiles):
        right_wide[t * few : (t + 1) * few] = (
            tile[:few].astype(jnp.float32).reshape(few, cols // 8, 8, width)
        )
    sum_many, sum_few = run_sums(many, cols), run_sums(few, 8)

    def of_rows(step, _):
        lines = [step * PAIR + n for n in range(PAIR)]
        narrow = [left_ref[line] for line in lines]
        wide = [left.astype(jnp.float32).reshape(cols // 8, 8, width) for left in narrow]
        for t, tile in enumerate(tiles):
            products = jnp.concatenate(
                [(tile[few:] * left[None]).reshape(many * cols, width) for left in narrow], axis=1
            )
            last = jnp.dot(sum_many, products, preferred_element_type=jnp.float32)
            partial = [0.0] * PAIR
            for k in range(cols // 8):
                right = right_wide[t * few : (t + 1) * few, k]
                partial = [total + right * left[k] for total, left in zip(partial, wide)]
            partial = [total.reshape(few * 8, width) for total in partial]
            first = jnp.dot(
                sum_few,
                jnp.concatenate(partial, axis=1).astype(jnp.bfloat16),
                preferred_element_type=jnp.float32,
            )
            sums = jnp.concatenate([first, last], axis=0)
            for n, line in enumerate(lines):
                place = (line, slice(t * rows, (t + 1) * rows))
                total = sums[:, n * width : (n + 1) * width]
                if more:
                    total = total + sum_ref[place]
                sum_ref[place] = total.astype(sum_ref.dtype)
        return 0

    lax.fori_loop(0, rows // PAIR, of_rows, 0, unroll=UNROLL)


def paired(sums):
    rows, cols, width = sums.shape
    pairs = sums.reshape(rows // 2, 2, cols, width)
    return jnp.concatenate([pairs[:, 0], pairs[:, 1]], axis=1)


def unpaired(pairs):
    half, double, width = pairs.shape
    cols = double // 2
    return jnp.stack([pairs[:, :cols], pairs[:, cols:]], axis=1).reshape(2 * half, cols, width)


def middle_kernel(
    flags_ref,
    left_ref,
    left_other,
    next_ref,
    pair_ref,
    kept_own,
    kept_other,
    sent_own,
    sent_other,
    both,
    right_wide,
):
    rows = left_ref.shape[0]
    keeps_near = flags_ref[3] == 1
    for left, kept, sent in ((left_ref, kept_own, sent_own), (left_other, kept_other, sent_other)):
        triangle(left, [next_ref, pair_ref], both, right_wide)
        of_next, of_pair = both[:, :rows], both[:, rows:]
        kept[...] = paired(jnp.where(keeps_near, of_next, of_pair)).astype(jnp.bfloat16)
        sent[...] = paired(jnp.where(keeps_near, of_pair, of_next)).astype(jnp.bfloat16)


def last_kernel(
    flags_ref, left_ref, given_ref, straight_ref, across_ref, sum_ref, right_wide
):
    @pl.when(flags_ref[3] == 0)
    def _():
        triangle(left_ref, [straight_ref], sum_ref, right_wide)
        triangle(given_ref, [across_ref], sum_ref, right_wide, more=True)


def finished(flags_ref, own, partner, at, gain_ref, proj_ref, gating_ref):
    rows, _, width = own.shape
    core = flags_ref[2] == 1
    hidden = jnp.concatenate(
        [jnp.where(core, partner, own), jnp.where(core, own, partner)], axis=1
    ).reshape(2 * rows * rows, width)
    normed = layer_norm(hidden, gain_ref[...]).astype(jnp.bfloat16)
    projected = jnp.dot(normed, proj_ref[...], preferred_element_type=jnp.float32)
    gating = jnp.where(at == 1, gating_ref[:, 2 * rows :], gating_ref[:, : 2 * rows])
    return gating * projected.reshape(rows, 2 * rows, width)


def swapped_kernel(
    flags_ref,
    own_ref,
    own_given,
    partner_ref,
    partner_given,
    gain_ref,
    proj_ref,
    gating_ref,
    out_ref,
):
    keeps_near, odd = flags_ref[3], flags_ref[4]
    total = lambda a, b: unpaired(a[...].astype(jnp.float32) + b[...].astype(jnp.float32))
    at = jnp.where(keeps_near == 1, 1 - odd, odd)
    out_ref[...] = finished(
        flags_ref,
        total(own_ref, own_given),
        total(partner_ref, partner_given),
        at,
        gain_ref,
        proj_ref,
        gating_ref,
    ).astype(jnp.bfloat16)


def finish_kernel(
    flags_ref,
    left_ref,
    given_ref,
    straight_ref,
    across_ref,
    mine_ref,
    near_ref,
    done_ref,
    gain_ref,
    proj_ref,
    gating_ref,
    out_ref,
    other_ref,
    right_wide,
):
    last_kernel(
        flags_ref, left_ref, given_ref, straight_ref, across_ref, other_ref, right_wide
    )
    rows = out_ref.shape[0]
    keeps_near, odd = flags_ref[3] == 1, flags_ref[4]
    near = near_ref[...].astype(jnp.float32) + given_ref[:, : 2 * rows].astype(jnp.float32)
    own = jnp.where(keeps_near, near[:, :rows], mine_ref[...])
    partner = jnp.where(keeps_near, near[:, rows:], other_ref[...])
    at = jnp.where(keeps_near, odd, 1 - odd)
    result = finished(flags_ref, own, partner, at, gain_ref, proj_ref, gating_ref)
    done = done_ref[...].astype(jnp.float32)
    out_ref[...] = jnp.concatenate(
        [jnp.where(at == 1, done, result), jnp.where(at == 1, result, done)], axis=1
    ).astype(jnp.bfloat16)


def call(kernel, micros, out_shape, scratch=()):
    vmem = pl.BlockSpec(memory_space=pltpu.VMEM)

    def run(flags, *arrays):
        return pl.pallas_call(
            kernel,
            out_shape=out_shape,
            in_specs=[pl.BlockSpec(memory_space=pltpu.SMEM)] + [vmem] * len(arrays),
            out_specs=jax.tree.map(lambda _: vmem, out_shape),
            scratch_shapes=list(scratch),
            compiler_params=pltpu.CompilerParams(vmem_limit_bytes=VMEM_LIMIT),
            cost_estimate=pl.CostEstimate(
                flops=int(micros * 1.1e9), bytes_accessed=int(micros * 3e6), transcendentals=0
            ),
        )(flags, *arrays)

    return run


def exchanged(
    pair_rep,
    residue_mask,
    ln_gain,
    left_proj,
    left_gate,
    right_proj,
    right_gate,
    hidden_gain,
    out_proj,
    out_gate,
):
    rows, cols, width = pair_rep.shape
    tile = rows * cols
    row = lax.axis_index("row")
    col = lax.axis_index("col")
    core = row % 2
    chip = row // 2
    keeps_near = (chip // 2 == col).astype(jnp.int32)
    flags = jnp.stack([row, col, core, keeps_near, chip % 2]).astype(jnp.int32)
    mask = residue_mask.reshape(1, -1)
    ln_gain = ln_gain.reshape(1, -1)
    hidden_gain = hidden_gain.reshape(1, -1)

    places = range(16)
    over_core = [(p, p ^ 2) for p in places]
    over_next = [(p, p ^ 4) for p in places]
    over_pair = [(p, p ^ 8) for p in places]
    over_col = [(p, p ^ 1) for p in places]
    over_both = [(p, p ^ 3) for p in places]
    keeps_far = lambda p: p // 8 != p % 2
    straight = [(p, p ^ 4) for p in places if keeps_far(p ^ 4)]
    across = [(p, p ^ 5) for p in places if keeps_far(p ^ 5)]
    send = lambda value, pairs: lax.ppermute(value, LINE, pairs)

    bf16 = lambda *shape: jax.ShapeDtypeStruct(shape, jnp.bfloat16)
    f32 = lambda *shape: jax.ShapeDtypeStruct(shape, jnp.float32)
    two, one = (rows, 2 * rows, width), (rows, rows, width)
    wide = lambda tiles: [pltpu.VMEM((tiles * VECTOR_ROWS, cols // 8, 8, width), jnp.float32)]
    right = call(right_kernel, 2.2, bf16(rows, cols, width))(
        flags, pair_rep, mask, ln_gain, right_proj, right_gate
    )

    from_pair = send(right, over_pair)
    from_next = send(right, over_next)
    from_core = send(right, over_core)

    after = lambda value, *last: lax.optimization_barrier((value, *last))[0]
    left, gating, near, swap, hidden_gain = call(
        left_kernel,
        4.0,
        (
            bf16(rows, cols, width),
            f32(tile, width),
            bf16(*two),
            bf16(rows, cols, width),
            f32(1, width),
        ),
        wide(2),
    )(flags, pair_rep, mask, ln_gain, left_proj, left_gate, out_gate, right, from_core, hidden_gain)
    given = send(swap, over_col)
    left_other = send(left, over_core)

    from_pair = after(from_pair, left)
    from_next = after(from_next, from_pair, given)
    far_straight, far_across = send(from_pair, straight), send(from_pair, across)
    kept_own, kept_other, sent_own, sent_other = call(
        middle_kernel,
        5.7,
        (bf16(rows // 2, 2 * rows, width),) * 4,
        [pltpu.VMEM(two, jnp.float32)] + wide(2),
    )(flags, left, after(left_other, from_pair), from_next, from_pair)
    kept_given = send(sent_own, over_col)
    partner_given = send(sent_other, over_both)
    partner = send(kept_other, over_core)

    far_straight, far_across = after(far_straight, kept_own), after(far_across, kept_own)
    other_straight, other_across = send(far_straight, over_core), send(far_across, over_core)
    mine = call(
        last_kernel, 0.1, f32(*one), wide(1)
    )(flags, left, given, far_straight, far_across)
    gating = gating.reshape(rows, cols, width)
    done = call(
        swapped_kernel,
        8.0,
        bf16(*two),
    )(flags, kept_own, kept_given, partner, partner_given, hidden_gain, out_proj, gating)
    other_straight, other_across = after(other_straight, done), after(other_across, done)
    return call(
        finish_kernel,
        4.0,
        bf16(rows, cols, width),
        [pltpu.VMEM(one, jnp.float32)] + wide(1),
    )(
        flags,
        left,
        given,
        other_straight,
        other_across,
        mine,
        near,
        done,
        hidden_gain,
        out_proj,
        gating,
    )


def solution(mesh):
    in_specs = (
        P(("groups", "row"), "col", None),
        P("groups"),
        P(),
        P(),
        P(),
        P(),
        P(),
        P(),
        P(),
        P(),
    )
    out_specs = P(("groups", "row"), ("col", "chan"), None)
    short = mesh.shape["row"] == 8 and mesh.shape["col"] == 2 and mesh.shape["chan"] == 1
    local = exchanged if short else gathered
    return jax.shard_map(local, mesh=mesh, in_specs=in_specs, out_specs=out_specs, check_vma=False)
```

```python
import functools

import jax
import jax.numpy as jnp
from jax import lax
from jax.experimental import pallas as pl
from jax.experimental.pallas import tpu as pltpu
from jax.sharding import PartitionSpec as P

LINE = ("row", "col")
VMEM_LIMIT = 48 * 1024 * 1024
VECTOR_ROWS = 16
PAIR = 2
UNROLL = 10


def layer_norm(values, gain):
    center = jnp.mean(values, axis=-1, keepdims=True)
    spread = jnp.mean(jnp.square(values - center), axis=-1, keepdims=True)
    return (values - center) * lax.rsqrt(spread + 1e-05) * gain


def gated_pair(normed_pair, matrices, pair_mask):
    tile_rows, tile_cols, pair_width = normed_pair.shape
    stacked = jnp.concatenate(matrices, axis=1)
    width = matrices[0].shape[1]
    projected = jnp.dot(
        normed_pair.reshape(tile_rows * tile_cols, pair_width),
        stacked,
        preferred_element_type=jnp.float32,
    )
    projected = projected.reshape(tile_rows, tile_cols, 4, width)
    masked = pair_mask[:, :, None]
    left_act = (masked * jax.nn.sigmoid(projected[:, :, 1]) * projected[:, :, 0]).astype(
        jnp.bfloat16
    )
    right_act = (masked * jax.nn.sigmoid(projected[:, :, 3]) * projected[:, :, 2]).astype(
        jnp.bfloat16
    )
    return (left_act, right_act)


def finish_output(normed_hidden, normed_pair, out_proj, out_gate):
    projected = jnp.einsum(
        "ijc,cd->ijd", normed_hidden, out_proj, preferred_element_type=jnp.float32
    )
    gating = jax.nn.sigmoid(
        jnp.einsum("ijc,cd->ijd", normed_pair, out_gate, preferred_element_type=jnp.float32)
    )
    return (gating * projected).astype(jnp.bfloat16)


def gathered(
    pair_rep,
    residue_mask,
    ln_gain,
    left_proj,
    left_gate,
    right_proj,
    right_gate,
    hidden_gain,
    out_proj,
    out_gate,
):
    tile_rows, tile_cols, pair_width = pair_rep.shape
    hidden_width = left_proj.shape[1]
    core_count = lax.axis_size("chan")
    core_index = lax.axis_index("chan")
    row_index = lax.axis_index("row")
    col_index = lax.axis_index("col")
    mask_float = residue_mask.astype(jnp.float32)
    row_mask = lax.dynamic_slice_in_dim(mask_float, row_index * tile_rows, tile_rows)
    core_cols = tile_cols // core_count
    matrices_all = (left_proj, left_gate, right_proj, right_gate)
    normed_pair = layer_norm(pair_rep.astype(jnp.float32), ln_gain).astype(jnp.bfloat16)
    col_mask = lax.dynamic_slice_in_dim(mask_float, col_index * tile_cols, tile_cols)
    pair_mask = row_mask[:, None] * col_mask[None, :]
    half_width = hidden_width // core_count
    matrices = tuple(
        (
            lax.dynamic_slice_in_dim(matrix, core_index * half_width, half_width, 1)
            for matrix in matrices_all
        )
    )
    left_act, right_act = gated_pair(normed_pair, matrices, pair_mask)
    partial_sums = jnp.einsum(
        "ikc,jkc->ijc",
        left_act,
        lax.all_gather(right_act, "row", axis=0, tiled=True),
        preferred_element_type=jnp.float32,
    )
    tri_sum = lax.psum_scatter(
        partial_sums.astype(jnp.bfloat16), "col", scatter_dimension=1, tiled=True
    ).astype(jnp.float32)
    full_hidden = lax.all_to_all(
        tri_sum.astype(jnp.bfloat16), "chan", split_axis=1, concat_axis=2, tiled=True
    ).astype(tri_sum.dtype)
    normed_hidden = layer_norm(full_hidden, hidden_gain).astype(jnp.bfloat16)
    own_pair = lax.dynamic_slice_in_dim(normed_pair, core_index * core_cols, core_cols, 1)
    return finish_output(normed_hidden, own_pair, out_proj, out_gate)


def normed_rows(pair_ref, gain_ref):
    rows, cols, width = pair_ref.shape
    values = pair_ref[...].astype(jnp.float32).reshape(rows * cols, width)
    return layer_norm(values, gain_ref[...]).astype(jnp.bfloat16)


def mask_block(mask_ref, flags_ref, rows, cols, width):
    first = flags_ref[0] * rows
    col_mask = jnp.zeros((1, cols), jnp.int32)
    for block in range(mask_ref.shape[1] // cols):
        part = mask_ref[:, block * cols : (block + 1) * cols]
        col_mask = jnp.where(flags_ref[1] == block, part, col_mask)
    spread = jnp.transpose(jnp.broadcast_to(col_mask.astype(jnp.float32), (width, cols)))
    lanes = lax.broadcasted_iota(jnp.int32, mask_ref.shape, 1)
    blocks = []
    for row in range(rows):
        present = jnp.sum(jnp.where(lanes == first + row, mask_ref[...], 0), axis=1, keepdims=True)
        blocks.append(spread * present.astype(jnp.float32))
    return jnp.concatenate(blocks, axis=0)


def right_kernel(flags_ref, pair_ref, mask_ref, gain_ref, proj_ref, gate_ref, right_ref):
    rows, cols, width = pair_ref.shape
    normed = normed_rows(pair_ref, gain_ref)
    masked = mask_block(mask_ref, flags_ref, rows, cols, width)
    stacked = jnp.concatenate([proj_ref[...], gate_ref[...]], axis=1)
    both = jnp.dot(normed, stacked, preferred_element_type=jnp.float32)
    act = masked * jax.nn.sigmoid(both[:, width:]) * both[:, :width]
    right_ref[...] = act.astype(jnp.bfloat16).reshape(rows, cols, width)


def left_kernel(
    flags_ref,
    pair_ref,
    mask_ref,
    gain_ref,
    proj_ref,
    gate_ref,
    out_gate_ref,
    mine_ref,
    other_ref,
    hidden_gain_ref,
    left_ref,
    gating_ref,
    sum_ref,
    swap_ref,
    held_gain_ref,
    right_wide,
):
    rows, cols, width = pair_ref.shape
    normed = normed_rows(pair_ref, gain_ref)
    masked = mask_block(mask_ref, flags_ref, rows, cols, width)
    stacked = jnp.concatenate([proj_ref[...], gate_ref[...]], axis=1)
    both = jnp.dot(normed, stacked, preferred_element_type=jnp.float32)
    act = masked * jax.nn.sigmoid(both[:, width:]) * both[:, :width]
    left_ref[...] = act.astype(jnp.bfloat16).reshape(rows, cols, width)
    gating_ref[...] = jax.nn.sigmoid(
        jnp.dot(normed, out_gate_ref[...], preferred_element_type=jnp.float32)
    )
    triangle(left_ref, [mine_ref, other_ref], sum_ref, right_wide)
    held_gain_ref[...] = hidden_gain_ref[...]
    keeps_near = flags_ref[3] == 1

    @pl.when(keeps_near)
    def _():
        swap_ref[...] = left_ref[...]

    @pl.when(jnp.logical_not(keeps_near))
    def _():
        swap_ref[:, : 2 * rows] = sum_ref[...]
        swap_ref[:, 2 * rows :] = jnp.zeros((rows, cols - 2 * rows, width), jnp.bfloat16)


def run_sums(count, length):
    row = lax.broadcasted_iota(jnp.int32, (count, count * length), 0) * length
    col = lax.broadcasted_iota(jnp.int32, (count, count * length), 1)
    return jnp.where((col >= row) & (col < row + length), 1.0, 0.0).astype(jnp.bfloat16)


def triangle(left_ref, tiles, sum_ref, right_wide, more=False):
    rows, cols, width = left_ref.shape
    few = VECTOR_ROWS
    many = rows - few
    for t, tile in enumerate(tiles):
        right_wide[t * few : (t + 1) * few] = (
            tile[:few].astype(jnp.float32).reshape(few, cols // 8, 8, width)
        )
    sum_many, sum_few = run_sums(many, cols), run_sums(few, 8)

    def of_rows(step, _):
        lines = [step * PAIR + n for n in range(PAIR)]
        narrow = [left_ref[line] for line in lines]
        wide = [left.astype(jnp.float32).reshape(cols // 8, 8, width) for left in narrow]
        for t, tile in enumerate(tiles):
            products = jnp.concatenate(
                [(tile[few:] * left[None]).reshape(many * cols, width) for left in narrow], axis=1
            )
            last = jnp.dot(sum_many, products, preferred_element_type=jnp.float32)
            partial = [0.0] * PAIR
            for k in range(cols // 8):
                right = right_wide[t * few : (t + 1) * few, k]
                partial = [total + right * left[k] for total, left in zip(partial, wide)]
            partial = [total.reshape(few * 8, width) for total in partial]
            first = jnp.dot(
                sum_few,
                jnp.concatenate(partial, axis=1).astype(jnp.bfloat16),
                preferred_element_type=jnp.float32,
            )
            sums = jnp.concatenate([first, last], axis=0)
            for n, line in enumerate(lines):
                place = (line, slice(t * rows, (t + 1) * rows))
                total = sums[:, n * width : (n + 1) * width]
                if more:
                    total = total + sum_ref[place]
                sum_ref[place] = total.astype(sum_ref.dtype)
        return 0

    lax.fori_loop(0, rows // PAIR, of_rows, 0, unroll=UNROLL)


def paired(sums):
    rows, cols, width = sums.shape
    pairs = sums.reshape(rows // 2, 2, cols, width)
    return jnp.concatenate([pairs[:, 0], pairs[:, 1]], axis=1)


def unpaired(pairs):
    half, double, width = pairs.shape
    cols = double // 2
    return jnp.stack([pairs[:, :cols], pairs[:, cols:]], axis=1).reshape(2 * half, cols, width)


def middle_kernel(
    flags_ref,
    left_ref,
    left_other,
    next_ref,
    pair_ref,
    kept_own,
    kept_other,
    sent_own,
    sent_other,
    both,
    right_wide,
):
    rows = left_ref.shape[0]
    keeps_near = flags_ref[3] == 1
    for left, kept, sent in ((left_ref, kept_own, sent_own), (left_other, kept_other, sent_other)):
        triangle(left, [next_ref, pair_ref], both, right_wide)
        of_next, of_pair = both[:, :rows], both[:, rows:]
        kept[...] = paired(jnp.where(keeps_near, of_next, of_pair)).astype(jnp.bfloat16)
        sent[...] = paired(jnp.where(keeps_near, of_pair, of_next)).astype(jnp.bfloat16)


def last_kernel(
    flags_ref, left_ref, given_ref, straight_ref, across_ref, sum_ref, right_wide
):
    @pl.when(flags_ref[3] == 0)
    def _():
        triangle(left_ref, [straight_ref], sum_ref, right_wide)
        triangle(given_ref, [across_ref], sum_ref, right_wide, more=True)


def finished(flags_ref, own, partner, at, gain_ref, proj_ref, gating_ref):
    rows, _, width = own.shape
    core = flags_ref[2] == 1
    hidden = jnp.concatenate(
        [jnp.where(core, partner, own), jnp.where(core, own, partner)], axis=1
    ).reshape(2 * rows * rows, width)
    normed = layer_norm(hidden, gain_ref[...]).astype(jnp.bfloat16)
    projected = jnp.dot(normed, proj_ref[...], preferred_element_type=jnp.float32)
    gating = jnp.where(at == 1, gating_ref[:, 2 * rows :], gating_ref[:, : 2 * rows])
    return gating * projected.reshape(rows, 2 * rows, width)


def swapped_kernel(
    flags_ref,
    own_ref,
    own_given,
    partner_ref,
    partner_given,
    gain_ref,
    proj_ref,
    gating_ref,
    out_ref,
):
    keeps_near, odd = flags_ref[3], flags_ref[4]
    total = lambda a, b: unpaired(a[...].astype(jnp.float32) + b[...].astype(jnp.float32))
    at = jnp.where(keeps_near == 1, 1 - odd, odd)
    out_ref[...] = finished(
        flags_ref,
        total(own_ref, own_given),
        total(partner_ref, partner_given),
        at,
        gain_ref,
        proj_ref,
        gating_ref,
    ).astype(jnp.bfloat16)


def finish_kernel(
    flags_ref,
    left_ref,
    given_ref,
    straight_ref,
    across_ref,
    mine_ref,
    near_ref,
    done_ref,
    gain_ref,
    proj_ref,
    gating_ref,
    out_ref,
    other_ref,
    right_wide,
):
    last_kernel(
        flags_ref, left_ref, given_ref, straight_ref, across_ref, other_ref, right_wide
    )
    rows = out_ref.shape[0]
    keeps_near, odd = flags_ref[3] == 1, flags_ref[4]
    near = near_ref[...].astype(jnp.float32) + given_ref[:, : 2 * rows].astype(jnp.float32)
    own = jnp.where(keeps_near, near[:, :rows], mine_ref[...])
    partner = jnp.where(keeps_near, near[:, rows:], other_ref[...])
    at = jnp.where(keeps_near, odd, 1 - odd)
    result = finished(flags_ref, own, partner, at, gain_ref, proj_ref, gating_ref)
    done = done_ref[...].astype(jnp.float32)
    out_ref[...] = jnp.concatenate(
        [jnp.where(at == 1, done, result), jnp.where(at == 1, result, done)], axis=1
    ).astype(jnp.bfloat16)


def call(kernel, micros, out_shape, scratch=()):
    vmem = pl.BlockSpec(memory_space=pltpu.VMEM)

    def run(flags, *arrays):
        return pl.pallas_call(
            kernel,
            out_shape=out_shape,
            in_specs=[pl.BlockSpec(memory_space=pltpu.SMEM)] + [vmem] * len(arrays),
            out_specs=jax.tree.map(lambda _: vmem, out_shape),
            scratch_shapes=list(scratch),
            compiler_params=pltpu.CompilerParams(vmem_limit_bytes=VMEM_LIMIT),
            cost_estimate=pl.CostEstimate(
                flops=int(micros * 1.1e9), bytes_accessed=int(micros * 3e6), transcendentals=0
            ),
        )(flags, *arrays)

    return run


def exchanged(
    pair_rep,
    residue_mask,
    ln_gain,
    left_proj,
    left_gate,
    right_proj,
    right_gate,
    hidden_gain,
    out_proj,
    out_gate,
):
    rows, cols, width = pair_rep.shape
    tile = rows * cols
    row = lax.axis_index("row")
    col = lax.axis_index("col")
    core = row % 2
    chip = row // 2
    keeps_near = (chip // 2 == col).astype(jnp.int32)
    flags = jnp.stack([row, col, core, keeps_near, chip % 2]).astype(jnp.int32)
    mask = residue_mask.reshape(1, -1)
    ln_gain = ln_gain.reshape(1, -1)
    hidden_gain = hidden_gain.reshape(1, -1)

    places = range(16)
    over_core = [(p, p ^ 2) for p in places]
    over_next = [(p, p ^ 4) for p in places]
    over_pair = [(p, p ^ 8) for p in places]
    over_col = [(p, p ^ 1) for p in places]
    over_both = [(p, p ^ 3) for p in places]
    keeps_far = lambda p: p // 8 != p % 2
    straight = [(p, p ^ 4 if keeps_far(p ^ 4) else p ^ 2) for p in places]
    across = [(p, p ^ 5 if keeps_far(p ^ 5) else p ^ 1) for p in places]
    send = lambda value, pairs: lax.ppermute(value, LINE, pairs)

    bf16 = lambda *shape: jax.ShapeDtypeStruct(shape, jnp.bfloat16)
    f32 = lambda *shape: jax.ShapeDtypeStruct(shape, jnp.float32)
    two, one = (rows, 2 * rows, width), (rows, rows, width)
    wide = lambda tiles: [pltpu.VMEM((tiles * VECTOR_ROWS, cols // 8, 8, width), jnp.float32)]
    right = call(right_kernel, 2.2, bf16(rows, cols, width))(
        flags, pair_rep, mask, ln_gain, right_proj, right_gate
    )

    from_pair = send(right, over_pair)
    from_next = send(right, over_next)
    from_core = send(right, over_core)

    after = lambda value, *last: lax.optimization_barrier((value, *last))[0]
    left, gating, near, swap, hidden_gain = call(
        left_kernel,
        4.0,
        (
            bf16(rows, cols, width),
            f32(tile, width),
            bf16(*two),
            bf16(rows, cols, width),
            f32(1, width),
        ),
        wide(2),
    )(flags, pair_rep, mask, ln_gain, left_proj, left_gate, out_gate, right, from_core, hidden_gain)
    given = send(swap, over_col)
    left_other = send(left, over_core)

    from_next = after(from_next, left)
    from_pair = after(from_pair, from_next, given)
    far_straight, far_across = send(from_pair, straight), send(from_pair, across)
    kept_own, kept_other, sent_own, sent_other = call(
        middle_kernel,
        5.7,
        (bf16(rows // 2, 2 * rows, width),) * 4,
        [pltpu.VMEM(two, jnp.float32)] + wide(2),
    )(flags, left, after(left_other, from_pair), from_next, from_pair)
    kept_given = send(sent_own, over_col)
    partner_given = send(sent_other, over_both)
    partner = send(kept_other, over_core)

    far_straight, far_across = after(far_straight, kept_own), after(far_across, kept_own)
    other_straight, other_across = send(far_straight, over_core), send(far_across, over_core)
    mine = call(
        last_kernel, 0.1, f32(*one), wide(1)
    )(flags, left, given, far_straight, far_across)
    gating = gating.reshape(rows, cols, width)
    done = call(
        swapped_kernel,
        8.0,
        bf16(*two),
    )(flags, after(kept_own, mine), kept_given, partner, partner_given, hidden_gain, out_proj, gating)
    other_straight, other_across = after(other_straight, done), after(other_across, done)
    return call(
        finish_kernel,
        4.0,
        bf16(rows, cols, width),
        [pltpu.VMEM(one, jnp.float32)] + wide(1),
    )(
        flags,
        left,
        given,
        other_straight,
        other_across,
        mine,
        near,
        done,
        hidden_gain,
        out_proj,
        gating,
    )


def solution(mesh):
    in_specs = (
        P(("groups", "row"), "col", None),
        P("groups"),
        P(),
        P(),
        P(),
        P(),
        P(),
        P(),
        P(),
        P(),
    )
    out_specs = P(("groups", "row"), ("col", "chan"), None)
    short = mesh.shape["row"] == 8 and mesh.shape["col"] == 2 and mesh.shape["chan"] == 1
    local = exchanged if short else gathered
    return jax.shard_map(local, mesh=mesh, in_specs=in_specs, out_specs=out_specs, check_vma=False)
```

```python
import functools

import jax
import jax.numpy as jnp
from jax import lax
from jax.experimental import pallas as pl
from jax.experimental.pallas import tpu as pltpu
from jax.sharding import PartitionSpec as P

LINE = ("row", "col")
VMEM_LIMIT = 48 * 1024 * 1024
VECTOR_ROWS = 16
PAIR = 2
UNROLL = 10


def layer_norm(values, gain):
    center = jnp.mean(values, axis=-1, keepdims=True)
    spread = jnp.mean(jnp.square(values - center), axis=-1, keepdims=True)
    return (values - center) * lax.rsqrt(spread + 1e-05) * gain


def gated_pair(normed_pair, matrices, pair_mask):
    tile_rows, tile_cols, pair_width = normed_pair.shape
    stacked = jnp.concatenate(matrices, axis=1)
    width = matrices[0].shape[1]
    projected = jnp.dot(
        normed_pair.reshape(tile_rows * tile_cols, pair_width),
        stacked,
        preferred_element_type=jnp.float32,
    )
    projected = projected.reshape(tile_rows, tile_cols, 4, width)
    masked = pair_mask[:, :, None]
    left_act = (masked * jax.nn.sigmoid(projected[:, :, 1]) * projected[:, :, 0]).astype(
        jnp.bfloat16
    )
    right_act = (masked * jax.nn.sigmoid(projected[:, :, 3]) * projected[:, :, 2]).astype(
        jnp.bfloat16
    )
    return (left_act, right_act)


def finish_output(normed_hidden, normed_pair, out_proj, out_gate):
    projected = jnp.einsum(
        "ijc,cd->ijd", normed_hidden, out_proj, preferred_element_type=jnp.float32
    )
    gating = jax.nn.sigmoid(
        jnp.einsum("ijc,cd->ijd", normed_pair, out_gate, preferred_element_type=jnp.float32)
    )
    return (gating * projected).astype(jnp.bfloat16)


def gathered(
    pair_rep,
    residue_mask,
    ln_gain,
    left_proj,
    left_gate,
    right_proj,
    right_gate,
    hidden_gain,
    out_proj,
    out_gate,
):
    tile_rows, tile_cols, pair_width = pair_rep.shape
    hidden_width = left_proj.shape[1]
    core_count = lax.axis_size("chan")
    core_index = lax.axis_index("chan")
    row_index = lax.axis_index("row")
    col_index = lax.axis_index("col")
    mask_float = residue_mask.astype(jnp.float32)
    row_mask = lax.dynamic_slice_in_dim(mask_float, row_index * tile_rows, tile_rows)
    core_cols = tile_cols // core_count
    matrices_all = (left_proj, left_gate, right_proj, right_gate)
    normed_pair = layer_norm(pair_rep.astype(jnp.float32), ln_gain).astype(jnp.bfloat16)
    col_mask = lax.dynamic_slice_in_dim(mask_float, col_index * tile_cols, tile_cols)
    pair_mask = row_mask[:, None] * col_mask[None, :]
    half_width = hidden_width // core_count
    matrices = tuple(
        (
            lax.dynamic_slice_in_dim(matrix, core_index * half_width, half_width, 1)
            for matrix in matrices_all
        )
    )
    left_act, right_act = gated_pair(normed_pair, matrices, pair_mask)
    partial_sums = jnp.einsum(
        "ikc,jkc->ijc",
        left_act,
        lax.all_gather(right_act, "row", axis=0, tiled=True),
        preferred_element_type=jnp.float32,
    )
    tri_sum = lax.psum_scatter(
        partial_sums.astype(jnp.bfloat16), "col", scatter_dimension=1, tiled=True
    ).astype(jnp.float32)
    full_hidden = lax.all_to_all(
        tri_sum.astype(jnp.bfloat16), "chan", split_axis=1, concat_axis=2, tiled=True
    ).astype(tri_sum.dtype)
    normed_hidden = layer_norm(full_hidden, hidden_gain).astype(jnp.bfloat16)
    own_pair = lax.dynamic_slice_in_dim(normed_pair, core_index * core_cols, core_cols, 1)
    return finish_output(normed_hidden, own_pair, out_proj, out_gate)


def normed_rows(pair_ref, gain_ref):
    rows, cols, width = pair_ref.shape
    values = pair_ref[...].astype(jnp.float32).reshape(rows * cols, width)
    return layer_norm(values, gain_ref[...]).astype(jnp.bfloat16)


def mask_block(mask_ref, flags_ref, rows, cols, width):
    first = flags_ref[0] * rows
    col_mask = jnp.zeros((1, cols), jnp.int32)
    for block in range(mask_ref.shape[1] // cols):
        part = mask_ref[:, block * cols : (block + 1) * cols]
        col_mask = jnp.where(flags_ref[1] == block, part, col_mask)
    spread = jnp.transpose(jnp.broadcast_to(col_mask.astype(jnp.float32), (width, cols)))
    lanes = lax.broadcasted_iota(jnp.int32, mask_ref.shape, 1)
    blocks = []
    for row in range(rows):
        present = jnp.sum(jnp.where(lanes == first + row, mask_ref[...], 0), axis=1, keepdims=True)
        blocks.append(spread * present.astype(jnp.float32))
    return jnp.concatenate(blocks, axis=0)


def right_kernel(flags_ref, pair_ref, mask_ref, gain_ref, proj_ref, gate_ref, right_ref):
    rows, cols, width = pair_ref.shape
    normed = normed_rows(pair_ref, gain_ref)
    masked = mask_block(mask_ref, flags_ref, rows, cols, width)
    stacked = jnp.concatenate([proj_ref[...], gate_ref[...]], axis=1)
    both = jnp.dot(normed, stacked, preferred_element_type=jnp.float32)
    act = masked * jax.nn.sigmoid(both[:, width:]) * both[:, :width]
    right_ref[...] = act.astype(jnp.bfloat16).reshape(rows, cols, width)


def left_kernel(
    flags_ref,
    pair_ref,
    mask_ref,
    gain_ref,
    proj_ref,
    gate_ref,
    out_gate_ref,
    mine_ref,
    other_ref,
    hidden_gain_ref,
    left_ref,
    gating_ref,
    sum_ref,
    swap_ref,
    held_gain_ref,
    wide_sums,
    right_wide,
):
    rows, cols, width = pair_ref.shape
    normed = normed_rows(pair_ref, gain_ref)
    masked = mask_block(mask_ref, flags_ref, rows, cols, width)
    stacked = jnp.concatenate([proj_ref[...], gate_ref[...]], axis=1)
    both = jnp.dot(normed, stacked, preferred_element_type=jnp.float32)
    act = masked * jax.nn.sigmoid(both[:, width:]) * both[:, :width]
    left_ref[...] = act.astype(jnp.bfloat16).reshape(rows, cols, width)
    gating_ref[...] = jax.nn.sigmoid(
        jnp.dot(normed, out_gate_ref[...], preferred_element_type=jnp.float32)
    )
    triangle(left_ref, [mine_ref, other_ref], wide_sums, right_wide)
    sum_ref[...] = wide_sums[...].astype(jnp.bfloat16)
    held_gain_ref[...] = hidden_gain_ref[...]
    keeps_near = flags_ref[3] == 1

    @pl.when(keeps_near)
    def _():
        swap_ref[...] = left_ref[...]

    @pl.when(jnp.logical_not(keeps_near))
    def _():
        rest = jnp.zeros((rows, cols - 2 * rows, width), jnp.float32)
        swap_ref[...] = jnp.concatenate([wide_sums[...], rest], axis=1).astype(jnp.bfloat16)


def run_sums(count, length):
    row = lax.broadcasted_iota(jnp.int32, (count, count * length), 0) * length
    col = lax.broadcasted_iota(jnp.int32, (count, count * length), 1)
    return jnp.where((col >= row) & (col < row + length), 1.0, 0.0).astype(jnp.bfloat16)


def triangle(left_ref, tiles, sum_ref, right_wide, more=False):
    rows, cols, width = left_ref.shape
    few = VECTOR_ROWS
    many = rows - few
    for t, tile in enumerate(tiles):
        right_wide[t * few : (t + 1) * few] = (
            tile[:few].astype(jnp.float32).reshape(few, cols // 8, 8, width)
        )
    sum_many, sum_few = run_sums(many, cols), run_sums(few, 8)

    def of_rows(step, _):
        lines = [step * PAIR + n for n in range(PAIR)]
        narrow = [left_ref[line] for line in lines]
        wide = [left.astype(jnp.float32).reshape(cols // 8, 8, width) for left in narrow]
        for t, tile in enumerate(tiles):
            products = jnp.concatenate(
                [(tile[few:] * left[None]).reshape(many * cols, width) for left in narrow], axis=1
            )
            last = jnp.dot(sum_many, products, preferred_element_type=jnp.float32)
            partial = [0.0] * PAIR
            for k in range(cols // 8):
                right = right_wide[t * few : (t + 1) * few, k]
                partial = [total + right * left[k] for total, left in zip(partial, wide)]
            partial = [total.reshape(few * 8, width) for total in partial]
            first = jnp.dot(
                sum_few,
                jnp.concatenate(partial, axis=1).astype(jnp.bfloat16),
                preferred_element_type=jnp.float32,
            )
            sums = jnp.concatenate([first, last], axis=0)
            for n, line in enumerate(lines):
                place = (line, slice(t * rows, (t + 1) * rows))
                total = sums[:, n * width : (n + 1) * width]
                if more:
                    total = total + sum_ref[place]
                sum_ref[place] = total.astype(sum_ref.dtype)
        return 0

    lax.fori_loop(0, rows // PAIR, of_rows, 0, unroll=UNROLL)


def paired(sums):
    rows, cols, width = sums.shape
    pairs = sums.reshape(rows // 2, 2, cols, width)
    return jnp.concatenate([pairs[:, 0], pairs[:, 1]], axis=1)


def unpaired(pairs):
    half, double, width = pairs.shape
    cols = double // 2
    return jnp.stack([pairs[:, :cols], pairs[:, cols:]], axis=1).reshape(2 * half, cols, width)


def middle_kernel(
    flags_ref,
    left_ref,
    left_other,
    next_ref,
    pair_ref,
    kept_own,
    kept_other,
    sent_own,
    sent_other,
    both,
    right_wide,
):
    rows = left_ref.shape[0]
    keeps_near = flags_ref[3] == 1
    for left, kept, sent in ((left_ref, kept_own, sent_own), (left_other, kept_other, sent_other)):
        triangle(left, [next_ref, pair_ref], both, right_wide)
        of_next, of_pair = both[:, :rows], both[:, rows:]
        kept[...] = paired(jnp.where(keeps_near, of_next, of_pair)).astype(jnp.bfloat16)
        sent[...] = paired(jnp.where(keeps_near, of_pair, of_next)).astype(jnp.bfloat16)


def last_kernel(
    flags_ref, left_ref, given_ref, straight_ref, across_ref, sum_ref, right_wide
):
    @pl.when(flags_ref[3] == 0)
    def _():
        triangle(left_ref, [straight_ref], sum_ref, right_wide)
        triangle(given_ref, [across_ref], sum_ref, right_wide, more=True)


def finished(flags_ref, own, partner, at, gain_ref, proj_ref, gating_ref):
    rows, _, width = own.shape
    core = flags_ref[2] == 1
    hidden = jnp.concatenate(
        [jnp.where(core, partner, own), jnp.where(core, own, partner)], axis=1
    ).reshape(2 * rows * rows, width)
    normed = layer_norm(hidden, gain_ref[...]).astype(jnp.bfloat16)
    projected = jnp.dot(normed, proj_ref[...], preferred_element_type=jnp.float32)
    gating = jnp.where(at == 1, gating_ref[:, 2 * rows :], gating_ref[:, : 2 * rows])
    return gating * projected.reshape(rows, 2 * rows, width)


def swapped_kernel(
    flags_ref,
    own_ref,
    own_given,
    partner_ref,
    partner_given,
    gain_ref,
    proj_ref,
    gating_ref,
    out_ref,
):
    keeps_near, odd = flags_ref[3], flags_ref[4]
    total = lambda a, b: unpaired(a[...].astype(jnp.float32) + b[...].astype(jnp.float32))
    at = jnp.where(keeps_near == 1, 1 - odd, odd)
    out_ref[...] = finished(
        flags_ref,
        total(own_ref, own_given),
        total(partner_ref, partner_given),
        at,
        gain_ref,
        proj_ref,
        gating_ref,
    ).astype(jnp.bfloat16)


def finish_kernel(
    flags_ref,
    left_ref,
    given_ref,
    straight_ref,
    across_ref,
    mine_ref,
    near_ref,
    done_ref,
    gain_ref,
    proj_ref,
    gating_ref,
    out_ref,
    other_ref,
    right_wide,
):
    last_kernel(
        flags_ref, left_ref, given_ref, straight_ref, across_ref, other_ref, right_wide
    )
    rows = out_ref.shape[0]
    keeps_near, odd = flags_ref[3] == 1, flags_ref[4]
    near = near_ref[...].astype(jnp.float32) + given_ref[...].astype(jnp.float32)[:, : 2 * rows]
    own = jnp.where(keeps_near, near[:, :rows], mine_ref[...])
    partner = jnp.where(keeps_near, near[:, rows:], other_ref[...])
    at = jnp.where(keeps_near, odd, 1 - odd)
    result = finished(flags_ref, own, partner, at, gain_ref, proj_ref, gating_ref)
    done = done_ref[...].astype(jnp.float32)
    out_ref[...] = jnp.concatenate(
        [jnp.where(at == 1, done, result), jnp.where(at == 1, result, done)], axis=1
    ).astype(jnp.bfloat16)


def call(kernel, micros, out_shape, scratch=()):
    vmem = pl.BlockSpec(memory_space=pltpu.VMEM)

    def run(flags, *arrays):
        return pl.pallas_call(
            kernel,
            out_shape=out_shape,
            in_specs=[pl.BlockSpec(memory_space=pltpu.SMEM)] + [vmem] * len(arrays),
            out_specs=jax.tree.map(lambda _: vmem, out_shape),
            scratch_shapes=list(scratch),
            compiler_params=pltpu.CompilerParams(vmem_limit_bytes=VMEM_LIMIT),
            cost_estimate=pl.CostEstimate(
                flops=int(micros * 1.1e9), bytes_accessed=int(micros * 3e6), transcendentals=0
            ),
        )(flags, *arrays)

    return run


def exchanged(
    pair_rep,
    residue_mask,
    ln_gain,
    left_proj,
    left_gate,
    right_proj,
    right_gate,
    hidden_gain,
    out_proj,
    out_gate,
):
    rows, cols, width = pair_rep.shape
    tile = rows * cols
    row = lax.axis_index("row")
    col = lax.axis_index("col")
    core = row % 2
    chip = row // 2
    keeps_near = (chip // 2 == col).astype(jnp.int32)
    flags = jnp.stack([row, col, core, keeps_near, chip % 2]).astype(jnp.int32)
    mask = residue_mask.reshape(1, -1)
    ln_gain = ln_gain.reshape(1, -1)
    hidden_gain = hidden_gain.reshape(1, -1)

    places = range(16)
    over_core = [(p, p ^ 2) for p in places]
    over_next = [(p, p ^ 4) for p in places]
    over_pair = [(p, p ^ 8) for p in places]
    over_col = [(p, p ^ 1) for p in places]
    over_both = [(p, p ^ 3) for p in places]
    keeps_far = lambda p: p // 8 != p % 2
    straight = [(p, p ^ 4 if keeps_far(p ^ 4) else p ^ 2) for p in places]
    across = [(p, p ^ 5 if keeps_far(p ^ 5) else p ^ 1) for p in places]
    send = lambda value, pairs: lax.ppermute(value, LINE, pairs)

    bf16 = lambda *shape: jax.ShapeDtypeStruct(shape, jnp.bfloat16)
    f32 = lambda *shape: jax.ShapeDtypeStruct(shape, jnp.float32)
    two, one = (rows, 2 * rows, width), (rows, rows, width)
    wide = lambda tiles: [pltpu.VMEM((tiles * VECTOR_ROWS, cols // 8, 8, width), jnp.float32)]
    right = call(right_kernel, 2.2, bf16(rows, cols, width))(
        flags, pair_rep, mask, ln_gain, right_proj, right_gate
    )

    from_pair = send(right, over_pair)
    from_next = send(right, over_next)
    from_core = send(right, over_core)

    after = lambda value, *last: lax.optimization_barrier((value, *last))[0]
    left, gating, near, swap, hidden_gain = call(
        left_kernel,
        4.0,
        (
            bf16(rows, cols, width),
            f32(tile, width),
            bf16(*two),
            bf16(rows, cols, width),
            f32(1, width),
        ),
        [pltpu.VMEM(two, jnp.float32)] + wide(2),
    )(flags, pair_rep, mask, ln_gain, left_proj, left_gate, out_gate, right, from_core, hidden_gain)
    given = send(swap, over_col)
    left_other = send(left, over_core)

    from_next = after(from_next, left)
    from_pair = after(from_pair, from_next, given)
    far_straight, far_across = send(from_pair, straight), send(from_pair, across)
    kept_own, kept_other, sent_own, sent_other = call(
        middle_kernel,
        5.7,
        (bf16(rows // 2, 2 * rows, width),) * 4,
        [pltpu.VMEM(two, jnp.float32)] + wide(2),
    )(flags, left, after(left_other, from_pair), from_next, from_pair)
    kept_given = send(sent_own, over_col)
    partner_given = send(sent_other, over_both)
    partner = send(kept_other, over_core)

    far_straight, far_across = after(far_straight, kept_own), after(far_across, kept_own)
    other_straight, other_across = send(far_straight, over_core), send(far_across, over_core)
    mine = call(
        last_kernel, 0.1, f32(*one), wide(1)
    )(flags, left, given, far_straight, far_across)
    gating = gating.reshape(rows, cols, width)
    done = call(
        swapped_kernel,
        8.0,
        bf16(*two),
    )(flags, after(kept_own, mine), kept_given, partner, partner_given, hidden_gain, out_proj, gating)
    other_straight, other_across = after(other_straight, done), after(other_across, done)
    return call(
        finish_kernel,
        4.0,
        bf16(rows, cols, width),
        [pltpu.VMEM(one, jnp.float32)] + wide(1),
    )(
        flags,
        left,
        given,
        other_straight,
        other_across,
        mine,
        near,
        done,
        hidden_gain,
        out_proj,
        gating,
    )


def solution(mesh):
    in_specs = (
        P(("groups", "row"), "col", None),
        P("groups"),
        P(),
        P(),
        P(),
        P(),
        P(),
        P(),
        P(),
        P(),
    )
    out_specs = P(("groups", "row"), ("col", "chan"), None)
    short = mesh.shape["row"] == 8 and mesh.shape["col"] == 2 and mesh.shape["chan"] == 1
    local = exchanged if short else gathered
    return jax.shard_map(local, mesh=mesh, in_specs=in_specs, out_specs=out_specs, check_vma=False)
```

```python
import functools

import jax
import jax.numpy as jnp
from jax import lax
from jax.experimental import pallas as pl
from jax.experimental.pallas import tpu as pltpu
from jax.sharding import PartitionSpec as P

LINE = ("row", "col")
VMEM_LIMIT = 48 * 1024 * 1024
VECTOR_ROWS = 12
PAIR = 2
UNROLL = 10


def layer_norm(values, gain):
    center = jnp.mean(values, axis=-1, keepdims=True)
    spread = jnp.mean(jnp.square(values - center), axis=-1, keepdims=True)
    return (values - center) * lax.rsqrt(spread + 1e-05) * gain


def gated_pair(normed_pair, matrices, pair_mask):
    tile_rows, tile_cols, pair_width = normed_pair.shape
    stacked = jnp.concatenate(matrices, axis=1)
    width = matrices[0].shape[1]
    projected = jnp.dot(
        normed_pair.reshape(tile_rows * tile_cols, pair_width),
        stacked,
        preferred_element_type=jnp.float32,
    )
    projected = projected.reshape(tile_rows, tile_cols, 4, width)
    masked = pair_mask[:, :, None]
    left_act = (masked * jax.nn.sigmoid(projected[:, :, 1]) * projected[:, :, 0]).astype(
        jnp.bfloat16
    )
    right_act = (masked * jax.nn.sigmoid(projected[:, :, 3]) * projected[:, :, 2]).astype(
        jnp.bfloat16
    )
    return (left_act, right_act)


def finish_output(normed_hidden, normed_pair, out_proj, out_gate):
    projected = jnp.einsum(
        "ijc,cd->ijd", normed_hidden, out_proj, preferred_element_type=jnp.float32
    )
    gating = jax.nn.sigmoid(
        jnp.einsum("ijc,cd->ijd", normed_pair, out_gate, preferred_element_type=jnp.float32)
    )
    return (gating * projected).astype(jnp.bfloat16)


def gathered(
    pair_rep,
    residue_mask,
    ln_gain,
    left_proj,
    left_gate,
    right_proj,
    right_gate,
    hidden_gain,
    out_proj,
    out_gate,
):
    tile_rows, tile_cols, pair_width = pair_rep.shape
    hidden_width = left_proj.shape[1]
    core_count = lax.axis_size("chan")
    core_index = lax.axis_index("chan")
    row_index = lax.axis_index("row")
    col_index = lax.axis_index("col")
    mask_float = residue_mask.astype(jnp.float32)
    row_mask = lax.dynamic_slice_in_dim(mask_float, row_index * tile_rows, tile_rows)
    core_cols = tile_cols // core_count
    matrices_all = (left_proj, left_gate, right_proj, right_gate)
    normed_pair = layer_norm(pair_rep.astype(jnp.float32), ln_gain).astype(jnp.bfloat16)
    col_mask = lax.dynamic_slice_in_dim(mask_float, col_index * tile_cols, tile_cols)
    pair_mask = row_mask[:, None] * col_mask[None, :]
    half_width = hidden_width // core_count
    matrices = tuple(
        (
            lax.dynamic_slice_in_dim(matrix, core_index * half_width, half_width, 1)
            for matrix in matrices_all
        )
    )
    left_act, right_act = gated_pair(normed_pair, matrices, pair_mask)
    partial_sums = jnp.einsum(
        "ikc,jkc->ijc",
        left_act,
        lax.all_gather(right_act, "row", axis=0, tiled=True),
        preferred_element_type=jnp.float32,
    )
    tri_sum = lax.psum_scatter(
        partial_sums.astype(jnp.bfloat16), "col", scatter_dimension=1, tiled=True
    ).astype(jnp.float32)
    full_hidden = lax.all_to_all(
        tri_sum.astype(jnp.bfloat16), "chan", split_axis=1, concat_axis=2, tiled=True
    ).astype(tri_sum.dtype)
    normed_hidden = layer_norm(full_hidden, hidden_gain).astype(jnp.bfloat16)
    own_pair = lax.dynamic_slice_in_dim(normed_pair, core_index * core_cols, core_cols, 1)
    return finish_output(normed_hidden, own_pair, out_proj, out_gate)


def normed_rows(pair_ref, gain_ref):
    rows, cols, width = pair_ref.shape
    values = pair_ref[...].astype(jnp.float32).reshape(rows * cols, width)
    return layer_norm(values, gain_ref[...]).astype(jnp.bfloat16)


def mask_block(mask_ref, flags_ref, rows, cols, width):
    first = flags_ref[0] * rows
    col_mask = jnp.zeros((1, cols), jnp.int32)
    for block in range(mask_ref.shape[1] // cols):
        part = mask_ref[:, block * cols : (block + 1) * cols]
        col_mask = jnp.where(flags_ref[1] == block, part, col_mask)
    spread = jnp.transpose(jnp.broadcast_to(col_mask.astype(jnp.float32), (width, cols)))
    lanes = lax.broadcasted_iota(jnp.int32, mask_ref.shape, 1)
    blocks = []
    for row in range(rows):
        present = jnp.sum(jnp.where(lanes == first + row, mask_ref[...], 0), axis=1, keepdims=True)
        blocks.append(spread * present.astype(jnp.float32))
    return jnp.concatenate(blocks, axis=0)


def right_kernel(flags_ref, pair_ref, mask_ref, gain_ref, proj_ref, gate_ref, right_ref):
    rows, cols, width = pair_ref.shape
    normed = normed_rows(pair_ref, gain_ref)
    masked = mask_block(mask_ref, flags_ref, rows, cols, width)
    stacked = jnp.concatenate([proj_ref[...], gate_ref[...]], axis=1)
    both = jnp.dot(normed, stacked, preferred_element_type=jnp.float32)
    act = masked * jax.nn.sigmoid(both[:, width:]) * both[:, :width]
    right_ref[...] = act.astype(jnp.bfloat16).reshape(rows, cols, width)


def left_kernel(
    flags_ref,
    pair_ref,
    mask_ref,
    gain_ref,
    proj_ref,
    gate_ref,
    out_gate_ref,
    mine_ref,
    other_ref,
    hidden_gain_ref,
    left_ref,
    gating_ref,
    sum_ref,
    swap_ref,
    held_gain_ref,
    wide_sums,
    right_wide,
):
    rows, cols, width = pair_ref.shape
    normed = normed_rows(pair_ref, gain_ref)
    masked = mask_block(mask_ref, flags_ref, rows, cols, width)
    stacked = jnp.concatenate([proj_ref[...], gate_ref[...]], axis=1)
    both = jnp.dot(normed, stacked, preferred_element_type=jnp.float32)
    act = masked * jax.nn.sigmoid(both[:, width:]) * both[:, :width]
    left_ref[...] = act.astype(jnp.bfloat16).reshape(rows, cols, width)
    gating_ref[...] = jax.nn.sigmoid(
        jnp.dot(normed, out_gate_ref[...], preferred_element_type=jnp.float32)
    )
    triangle(left_ref, [mine_ref, other_ref], wide_sums, right_wide)
    sum_ref[...] = wide_sums[...].astype(jnp.bfloat16)
    held_gain_ref[...] = hidden_gain_ref[...]
    keeps_near = flags_ref[3] == 1

    @pl.when(keeps_near)
    def _():
        swap_ref[...] = left_ref[...]

    @pl.when(jnp.logical_not(keeps_near))
    def _():
        rest = jnp.zeros((rows, cols - 2 * rows, width), jnp.float32)
        swap_ref[...] = jnp.concatenate([wide_sums[...], rest], axis=1).astype(jnp.bfloat16)


def run_sums(count, length):
    row = lax.broadcasted_iota(jnp.int32, (count, count * length), 0) * length
    col = lax.broadcasted_iota(jnp.int32, (count, count * length), 1)
    return jnp.where((col >= row) & (col < row + length), 1.0, 0.0).astype(jnp.bfloat16)


def triangle(left_ref, tiles, sum_ref, right_wide, more=False):
    rows, cols, width = left_ref.shape
    few = VECTOR_ROWS
    many = rows - few
    for t, tile in enumerate(tiles):
        right_wide[t * few : (t + 1) * few] = (
            tile[:few].astype(jnp.float32).reshape(few, cols // 8, 8, width)
        )
    sum_many, sum_few = run_sums(many, cols), run_sums(few, 8)

    def of_rows(step, _):
        lines = [step * PAIR + n for n in range(PAIR)]
        narrow = [left_ref[line] for line in lines]
        wide = [left.astype(jnp.float32).reshape(cols // 8, 8, width) for left in narrow]
        for t, tile in enumerate(tiles):
            products = jnp.concatenate(
                [(tile[few:] * left[None]).reshape(many * cols, width) for left in narrow], axis=1
            )
            last = jnp.dot(sum_many, products, preferred_element_type=jnp.float32)
            partial = [0.0] * PAIR
            for k in range(cols // 8):
                right = right_wide[t * few : (t + 1) * few, k]
                partial = [total + right * left[k] for total, left in zip(partial, wide)]
            partial = [total.reshape(few * 8, width) for total in partial]
            first = jnp.dot(
                sum_few,
                jnp.concatenate(partial, axis=1).astype(jnp.bfloat16),
                preferred_element_type=jnp.float32,
            )
            sums = jnp.concatenate([first, last], axis=0)
            for n, line in enumerate(lines):
                place = (line, slice(t * rows, (t + 1) * rows))
                total = sums[:, n * width : (n + 1) * width]
                if more:
                    total = total + sum_ref[place]
                sum_ref[place] = total.astype(sum_ref.dtype)
        return 0

    lax.fori_loop(0, rows // PAIR, of_rows, 0, unroll=UNROLL)


def paired(sums):
    rows, cols, width = sums.shape
    pairs = sums.reshape(rows // 2, 2, cols, width)
    return jnp.concatenate([pairs[:, 0], pairs[:, 1]], axis=1)


def unpaired(pairs):
    half, double, width = pairs.shape
    cols = double // 2
    return jnp.stack([pairs[:, :cols], pairs[:, cols:]], axis=1).reshape(2 * half, cols, width)


def middle_kernel(
    flags_ref,
    left_ref,
    left_other,
    next_ref,
    pair_ref,
    kept_own,
    kept_other,
    sent_own,
    sent_other,
    both,
    right_wide,
):
    rows = left_ref.shape[0]
    keeps_near = flags_ref[3] == 1
    for left, kept, sent in ((left_ref, kept_own, sent_own), (left_other, kept_other, sent_other)):
        triangle(left, [next_ref, pair_ref], both, right_wide)
        of_next, of_pair = both[:, :rows], both[:, rows:]
        kept[...] = paired(jnp.where(keeps_near, of_next, of_pair)).astype(jnp.bfloat16)
        sent[...] = paired(jnp.where(keeps_near, of_pair, of_next)).astype(jnp.bfloat16)


def last_kernel(
    flags_ref, left_ref, given_ref, straight_ref, across_ref, sum_ref, right_wide
):
    @pl.when(flags_ref[3] == 0)
    def _():
        triangle(left_ref, [straight_ref], sum_ref, right_wide)
        triangle(given_ref, [across_ref], sum_ref, right_wide, more=True)


def finished(flags_ref, own, partner, at, gain_ref, proj_ref, gating_ref):
    rows, _, width = own.shape
    core = flags_ref[2] == 1
    hidden = jnp.concatenate(
        [jnp.where(core, partner, own), jnp.where(core, own, partner)], axis=1
    ).reshape(2 * rows * rows, width)
    normed = layer_norm(hidden, gain_ref[...]).astype(jnp.bfloat16)
    projected = jnp.dot(normed, proj_ref[...], preferred_element_type=jnp.float32)
    gating = jnp.where(at == 1, gating_ref[:, 2 * rows :], gating_ref[:, : 2 * rows])
    return gating * projected.reshape(rows, 2 * rows, width)


def swapped_kernel(
    flags_ref,
    own_ref,
    own_given,
    partner_ref,
    partner_given,
    gain_ref,
    proj_ref,
    gating_ref,
    out_ref,
):
    keeps_near, odd = flags_ref[3], flags_ref[4]
    total = lambda a, b: unpaired(a[...].astype(jnp.float32) + b[...].astype(jnp.float32))
    at = jnp.where(keeps_near == 1, 1 - odd, odd)
    out_ref[...] = finished(
        flags_ref,
        total(own_ref, own_given),
        total(partner_ref, partner_given),
        at,
        gain_ref,
        proj_ref,
        gating_ref,
    ).astype(jnp.bfloat16)


def finish_kernel(
    flags_ref,
    left_ref,
    given_ref,
    straight_ref,
    across_ref,
    mine_ref,
    near_ref,
    done_ref,
    gain_ref,
    proj_ref,
    gating_ref,
    out_ref,
    other_ref,
    right_wide,
):
    last_kernel(
        flags_ref, left_ref, given_ref, straight_ref, across_ref, other_ref, right_wide
    )
    rows = out_ref.shape[0]
    keeps_near, odd = flags_ref[3] == 1, flags_ref[4]
    near = near_ref[...].astype(jnp.float32) + given_ref[...].astype(jnp.float32)[:, : 2 * rows]
    own = jnp.where(keeps_near, near[:, :rows], mine_ref[...])
    partner = jnp.where(keeps_near, near[:, rows:], other_ref[...])
    at = jnp.where(keeps_near, odd, 1 - odd)
    result = finished(flags_ref, own, partner, at, gain_ref, proj_ref, gating_ref)
    done = done_ref[...].astype(jnp.float32)
    out_ref[...] = jnp.concatenate(
        [jnp.where(at == 1, done, result), jnp.where(at == 1, result, done)], axis=1
    ).astype(jnp.bfloat16)


def call(kernel, micros, out_shape, scratch=()):
    vmem = pl.BlockSpec(memory_space=pltpu.VMEM)

    def run(flags, *arrays):
        return pl.pallas_call(
            kernel,
            out_shape=out_shape,
            in_specs=[pl.BlockSpec(memory_space=pltpu.SMEM)] + [vmem] * len(arrays),
            out_specs=jax.tree.map(lambda _: vmem, out_shape),
            scratch_shapes=list(scratch),
            compiler_params=pltpu.CompilerParams(vmem_limit_bytes=VMEM_LIMIT),
            cost_estimate=pl.CostEstimate(
                flops=int(micros * 1.1e9), bytes_accessed=int(micros * 3e6), transcendentals=0
            ),
        )(flags, *arrays)

    return run


def exchanged(
    pair_rep,
    residue_mask,
    ln_gain,
    left_proj,
    left_gate,
    right_proj,
    right_gate,
    hidden_gain,
    out_proj,
    out_gate,
):
    rows, cols, width = pair_rep.shape
    tile = rows * cols
    row = lax.axis_index("row")
    col = lax.axis_index("col")
    core = row % 2
    chip = row // 2
    keeps_near = (chip // 2 == col).astype(jnp.int32)
    flags = jnp.stack([row, col, core, keeps_near, chip % 2]).astype(jnp.int32)
    mask = residue_mask.reshape(1, -1)
    ln_gain = ln_gain.reshape(1, -1)
    hidden_gain = hidden_gain.reshape(1, -1)

    places = range(16)
    over_core = [(p, p ^ 2) for p in places]
    over_next = [(p, p ^ 4) for p in places]
    over_pair = [(p, p ^ 8) for p in places]
    over_col = [(p, p ^ 1) for p in places]
    over_both = [(p, p ^ 3) for p in places]
    keeps_far = lambda p: p // 8 != p % 2
    straight = [(p, p ^ 4 if keeps_far(p ^ 4) else p ^ 2) for p in places]
    across = [(p, p ^ 5 if keeps_far(p ^ 5) else p ^ 1) for p in places]
    send = lambda value, pairs: lax.ppermute(value, LINE, pairs)

    bf16 = lambda *shape: jax.ShapeDtypeStruct(shape, jnp.bfloat16)
    f32 = lambda *shape: jax.ShapeDtypeStruct(shape, jnp.float32)
    two, one = (rows, 2 * rows, width), (rows, rows, width)
    wide = lambda tiles: [pltpu.VMEM((tiles * VECTOR_ROWS, cols // 8, 8, width), jnp.float32)]
    right = call(right_kernel, 2.2, bf16(rows, cols, width))(
        flags, pair_rep, mask, ln_gain, right_proj, right_gate
    )

    from_pair = send(right, over_pair)
    from_next = send(right, over_next)
    from_core = send(right, over_core)

    after = lambda value, *last: lax.optimization_barrier((value, *last))[0]
    left, gating, near, swap, hidden_gain = call(
        left_kernel,
        4.0,
        (
            bf16(rows, cols, width),
            f32(tile, width),
            bf16(*two),
            bf16(rows, cols, width),
            f32(1, width),
        ),
        [pltpu.VMEM(two, jnp.float32)] + wide(2),
    )(flags, pair_rep, mask, ln_gain, left_proj, left_gate, out_gate, right, from_core, hidden_gain)
    given = send(swap, over_col)
    left_other = send(left, over_core)

    from_next = after(from_next, left)
    from_pair = after(from_pair, from_next, given)
    far_straight, far_across = send(from_pair, straight), send(from_pair, across)
    kept_own, kept_other, sent_own, sent_other = call(
        middle_kernel,
        5.7,
        (bf16(rows // 2, 2 * rows, width),) * 4,
        [pltpu.VMEM(two, jnp.float32)] + wide(2),
    )(flags, left, after(left_other, from_pair), from_next, from_pair)
    kept_given = send(sent_own, over_col)
    partner_given = send(sent_other, over_both)
    partner = send(kept_other, over_core)

    far_straight, far_across = after(far_straight, kept_own), after(far_across, kept_own)
    other_straight, other_across = send(far_straight, over_core), send(far_across, over_core)
    mine = call(
        last_kernel, 0.1, f32(*one), wide(1)
    )(flags, left, given, far_straight, far_across)
    gating = gating.reshape(rows, cols, width)
    done = call(
        swapped_kernel,
        8.0,
        bf16(*two),
    )(flags, after(kept_own, mine), kept_given, partner, partner_given, hidden_gain, out_proj, gating)
    other_straight, other_across = after(other_straight, done), after(other_across, done)
    return call(
        finish_kernel,
        4.0,
        bf16(rows, cols, width),
        [pltpu.VMEM(one, jnp.float32)] + wide(1),
    )(
        flags,
        left,
        given,
        other_straight,
        other_across,
        mine,
        near,
        done,
        hidden_gain,
        out_proj,
        gating,
    )


def solution(mesh):
    in_specs = (
        P(("groups", "row"), "col", None),
        P("groups"),
        P(),
        P(),
        P(),
        P(),
        P(),
        P(),
        P(),
        P(),
    )
    out_specs = P(("groups", "row"), ("col", "chan"), None)
    short = mesh.shape["row"] == 8 and mesh.shape["col"] == 2 and mesh.shape["chan"] == 1
    local = exchanged if short else gathered
    return jax.shard_map(local, mesh=mesh, in_specs=in_specs, out_specs=out_specs, check_vma=False)
```
